256 devices in a mesh: blk: 32 (over z, x_lo, core), group: 8 (over y, x_hi).
Axes of the slice: x: 4 (x_hi: 2, x_lo: 2; x = x_hi * 2 + x_lo), y: 4, z: 8, core: 2. Of those that a mesh axis runs over, the one named last changes fastest.
Arguments:
- picture_pooled_states: bfloat16 [65536, 1536], P(('blk', 'group')), may hold values from -6 to 6
- caption_pooled_states: bfloat16 [65536, 1536], P(('blk', 'group')), may hold values from -6 to 6
- picture_rescale_factor: float32 [1536], replicated, may hold values from 0.1 to 1.9
- caption_rescale_factor: float32 [1536], replicated, may hold values from 0.1 to 1.9
- picture_head_matrix: bfloat16 [1536, 1024], replicated, may hold values from -0.15625 to 0.15625
- caption_head_matrix: bfloat16 [1536, 1024], replicated, may hold values from -0.15625 to 0.15625
- sharpness_factor: float32 [1], replicated, may hold values from 30 to 100
- score_offset_term: float32 [1], replicated, may hold values from -10 to -5
Outputs:
- image_feature_gradient: float32 [65536, 1536], P(('blk', 'group'))
- text_feature_gradient: float32 [65536, 1536], P(('blk', 'group'))
- img_weight_grad: float32 [1536, 1024], P('blk', 'group')
- txt_weight_grad: float32 [1536, 1024], P('blk', 'group')
The draws below stay inside these ranges and needn't reach their ends.
All inputs are finite; a program needn't handle non-finite values.
Results may differ from the reference program's by a relative error of at most 0.025.
Values may be sent and summed in bfloat16 or wider, within the bound.
A program may use at most 128 MiB of HBM per device.

```python
import math
import jax
import jax.numpy as jnp
from jax import lax

D = 1536
E = 1024
GROUP_ROWS = 2048
BATCH = 65536
N_BLK = 32


def levels(own_key, shape, split, smallest, largest):
    level = 1.0
    for dim, blocks in split:
        draws = jax.random.uniform(jax.random.fold_in(jax.random.fold_in(own_key, 6), dim), (blocks,), jnp.float32, smallest / len(split), largest / len(split))
        level = level * jnp.repeat(jnp.exp(draws), shape[dim] // blocks).reshape((-1,) + (1,) * (len(shape) - 1 - dim))
    return level


def normal_values(rng, dims, width, bound, split=(), held_as=jnp.bfloat16):
    result = width * jax.random.normal(rng, dims, jnp.float32)
    if split:
        result = result * levels(rng, dims, split, -0.22, 0.18)
    return jnp.clip(result, -bound, bound).astype(held_as)


def setup_inputs(seed: int = 0) -> dict:
    key_of = jax.random.split(jax.random.key(seed), 9)
    picture_pooled_states = normal_values(key_of[0], (BATCH, D), 1.0, 6.0, ((0, 256),))
    caption_pooled_states = normal_values(key_of[1], (BATCH, D), 1.0, 6.0, ((0, 256),))
    picture_rescale_factor = jnp.clip(1.0 + 0.18 * jax.random.normal(key_of[2], (D,), jnp.float32), 0.1, 1.9)
    caption_rescale_factor = jnp.clip(1.0 + 0.18 * jax.random.normal(key_of[3], (D,), jnp.float32), 0.1, 1.9)
    picture_head_matrix = normal_values(key_of[4], (D, E), D ** -0.5, 0.15625)
    caption_head_matrix = normal_values(key_of[5], (D, E), D ** -0.5, 0.15625)
    sharpness_factor = jnp.clip(jnp.exp(jax.random.uniform(key_of[6], (1,), jnp.float32, math.log(30.0), math.log(100.0))), 30.0, 100.0)
    score_offset_term = jnp.clip(jax.random.uniform(key_of[7], (1,), jnp.float32, -10.0, -5.0), -10.0, -5.0)
    return {"picture_pooled_states": picture_pooled_states, "caption_pooled_states": caption_pooled_states, "picture_rescale_factor": picture_rescale_factor, "caption_rescale_factor": caption_rescale_factor, "picture_head_matrix": picture_head_matrix, "caption_head_matrix": caption_head_matrix, "sharpness_factor": sharpness_factor, "score_offset_term": score_offset_term}


def projection_forward(feats, norm_gain, projection_weight):
    values = feats.astype(jnp.float32)
    feature_average = lax.optimization_barrier(jnp.mean(values, axis=-1, keepdims=True))
    centered_input = values - feature_average
    inverse_deviation = lax.rsqrt(lax.optimization_barrier(jnp.mean(centered_input * centered_input, axis=-1, keepdims=True)) + 1e-06)
    normalized_input = centered_input * inverse_deviation
    activation = (normalized_input * norm_gain).astype(jnp.bfloat16)
    proj = jnp.dot(activation, projection_weight, preferred_element_type=jnp.float32)
    inverse_norm = lax.rsqrt(lax.optimization_barrier(jnp.sum(proj * proj, axis=-1, keepdims=True)) + 1e-06)
    unit_vector = proj * inverse_norm
    return (normalized_input, inverse_deviation, activation, unit_vector, inverse_norm, unit_vector.astype(jnp.bfloat16))

def projection_backward(embedding_gradient, norm_gain, projection_weight, normalized_input, inverse_deviation, activation, unit_vector, inverse_norm):
    dproj = ((embedding_gradient - unit_vector * lax.optimization_barrier(jnp.sum(unit_vector * embedding_gradient, axis=-1, keepdims=True))) * inverse_norm).astype(jnp.bfloat16)
    d_act = jnp.dot(dproj, projection_weight.T, preferred_element_type=jnp.float32)
    normalized_gradient = d_act * norm_gain
    feature_gradient = inverse_deviation * (normalized_gradient - lax.optimization_barrier(jnp.mean(normalized_gradient, axis=-1, keepdims=True)) - normalized_input * lax.optimization_barrier(jnp.mean(normalized_gradient * normalized_input, axis=-1, keepdims=True)))
    w_grad = jnp.dot(activation.T, dproj, preferred_element_type=jnp.float32)
    return (feature_gradient, w_grad)

def matched_tile(picture_latents, caption_latents, starting_position, sharpness_parameter, displacement_amount, matching_label):
    similarity_matrix = jnp.dot(picture_latents, caption_latents.T, preferred_element_type=jnp.float32)
    sigmoid_likelihood = jax.nn.sigmoid(sharpness_parameter * similarity_matrix + displacement_amount)
    if matching_label:
        row_ids = jnp.arange(picture_latents.shape[0], dtype=jnp.int32)[:, None] + starting_position
        col_ids = jnp.arange(caption_latents.shape[0], dtype=jnp.int32)[None, :]
        sigmoid_likelihood = sigmoid_likelihood - (row_ids == col_ids).astype(jnp.float32)
    pairwise_multiplier = sigmoid_likelihood.astype(jnp.bfloat16)
    picture_side_derivs = sharpness_parameter * jnp.dot(pairwise_multiplier, caption_latents, preferred_element_type=jnp.float32)
    caption_side_derivs = sharpness_parameter * jnp.dot(pairwise_multiplier.T, picture_latents, preferred_element_type=jnp.float32)
    return (picture_side_derivs, caption_side_derivs)

def reference(picture_pooled_states, caption_pooled_states, picture_rescale_factor, caption_rescale_factor, picture_head_matrix, caption_head_matrix, sharpness_factor, score_offset_term):
    sharpness_parameter = sharpness_factor[0]
    displacement_amount = score_offset_term[0]
    image_normalized_input, image_inverse_std, image_activation, image_unit_vector, image_inverse_norm, picture_latent = projection_forward(picture_pooled_states, picture_rescale_factor, picture_head_matrix)
    text_normalized_input, text_inverse_std, text_activation, text_unit_vector, text_inverse_norm, text_embedding = projection_forward(caption_pooled_states, caption_rescale_factor, caption_head_matrix)

    def visit(carry, index):
        start = (index * GROUP_ROWS).astype(jnp.int32)
        before = ((index + N_BLK - 1) % N_BLK * GROUP_ROWS).astype(jnp.int32)
        picture_latents = lax.dynamic_slice_in_dim(picture_latent, start, GROUP_ROWS, 0)
        local_caption_batch = lax.dynamic_slice_in_dim(text_embedding, start, GROUP_ROWS, 0)
        remote_caption_batch = lax.dynamic_slice_in_dim(text_embedding, before, GROUP_ROWS, 0)
        local_picture_share, local_caption_share = matched_tile(picture_latents, local_caption_batch, 0, sharpness_parameter, displacement_amount, True)
        remote_picture_share, remote_caption_share = matched_tile(picture_latents, remote_caption_batch, 0, sharpness_parameter, displacement_amount, False)
        carry = lax.dynamic_update_slice_in_dim(carry, lax.dynamic_slice_in_dim(carry, start, GROUP_ROWS, 0) + local_caption_share, start, 0)
        carry = lax.dynamic_update_slice_in_dim(carry, lax.dynamic_slice_in_dim(carry, before, GROUP_ROWS, 0) + remote_caption_share, before, 0)
        return (carry, local_picture_share + remote_picture_share)
    text_embedding_gradient, d_img_blocks = lax.scan(visit, jnp.zeros((BATCH, E), jnp.float32), jnp.arange(N_BLK, dtype=jnp.int32))
    image_embedding_gradient = d_img_blocks.reshape(BATCH, E)
    image_feature_gradient, image_weight_gradient = projection_backward(image_embedding_gradient, picture_rescale_factor, picture_head_matrix, image_normalized_input, image_inverse_std, image_activation, image_unit_vector, image_inverse_norm)
    text_feature_gradient, text_weight_gradient = projection_backward(text_embedding_gradient, caption_rescale_factor, caption_head_matrix, text_normalized_input, text_inverse_std, text_activation, text_unit_vector, text_inverse_norm)
    scale = math.sqrt(E / BATCH)
    return (image_feature_gradient, text_feature_gradient, image_weight_gradient * scale, text_weight_gradient * scale)
```

```python
import functools
import math

import jax
import jax.numpy as jnp
from jax import lax
from jax.experimental import pallas as pl
from jax.experimental.pallas import tpu as pltpu
from jax.sharding import PartitionSpec as P

BF = jnp.bfloat16
F32 = jnp.float32
NT = (((1,), (1,)), ((), ()))
TN = (((0,), (0,)), ((), ()))


def device_at(x, y, z, c):
    x, y, z = lax.rem(x, 4), lax.rem(y, 4), lax.rem(z, 8)
    return {"blk": z * 4 + lax.rem(x, 2) * 2 + c, "group": y * 2 + x // 2}


def remote(src, dst, send, recv, device):
    return pltpu.make_async_remote_copy(
        src_ref=src,
        dst_ref=dst,
        send_sem=send,
        recv_sem=recv,
        device_id=device,
        device_id_type=pl.DeviceIdType.MESH,
    )


def landed(ref, sem):
    pltpu.make_async_copy(ref, ref, sem).wait()


def kernel(
    scale,
    sharp_ref,
    off_ref,
    gain_i,
    gain_t,
    feat_i,
    feat_t,
    w_i,
    w_t,
    gi_out,
    gt_out,
    wi_out,
    wt_out,
    feats,
    weights,
    gains,
    act,
    act_t,
    unit,
    inv_norm,
    mean_s,
    rstd_s,
    imgs,
    txts,
    coef,
    d_own,
    d_txt,
    di_send,
    di_recv,
    dt_send,
    dt_recv,
    dp,
    d_act,
    wb,
    wr1,
    s1,
    wr2,
    s2,
    wr3,
    fin,
    load_sem,
    i_send,
    i_recv,
    t_send,
    t_recv,
    a_sem,
    di_ss,
    di_rs,
    dt_ss,
    dt_rs,
    dp_sem,
    w1_ss,
    w1_rs,
    w2_ss,
    w2_rs,
    w3_ss,
    w3_rs,
    f_sem,
):
    k = lax.axis_index("blk")
    g = lax.axis_index("group")
    c = lax.rem(k, 2)
    z = k // 4
    xl = lax.rem(k // 2, 2)
    y = g // 2
    xh = lax.rem(g, 2)
    x = 2 * xh + xl
    oc = 1 - c
    ox = 1 - xh
    other = {"blk": k + 1 - 2 * c, "group": g}
    partner = {"blk": k, "group": y * 2 + ox}
    behind = lax.rem(k + 31, 32)
    ahead = lax.rem(k + 1, 32)
    linked = lax.rem(k + 31 + 2 * c, 32)
    rows, width = feats.shape[1], feats.shape[2]
    emb = imgs.shape[2]

    loads = [
        pltpu.make_async_copy(feat_t, feats.at[1], load_sem.at[0]),
        pltpu.make_async_copy(w_t, weights.at[1], load_sem.at[1]),
        pltpu.make_async_copy(feat_i, feats.at[0], load_sem.at[2]),
        pltpu.make_async_copy(w_i, weights.at[0], load_sem.at[3]),
    ]
    for load in loads:
        load.start()

    barrier = pltpu.get_barrier_semaphore()
    partners = [device_at(x, y + d, z, c) for d in (1, 2, 3)]
    partners += [device_at(x + d, y, z, c) for d in (1, 2, 3)]
    partners += [device_at(x, y, z + d, c) for d in range(1, 8)]
    partners += [other]
    partners += [{"blk": linked, "group": y * 2 + j} for j in (0, 1)]
    for device in partners:
        pl.semaphore_signal(
            barrier, inc=1, device_id=device, device_id_type=pl.DeviceIdType.MESH
        )
    gains[0] = gain_i[...]
    gains[1] = gain_t[...]

    step = 32

    def normalize(t, wait_features):
        wait_features.wait()
        place = jnp.where(c == t, 0, 2)

        def body(i, _):
            r = pl.ds(pl.multiple_of(i * step, step), step)
            v = feats[t, r, :].astype(F32)
            mu = jnp.mean(v, axis=-1, keepdims=True)
            cen = v - mu
            rstd = lax.rsqrt(jnp.mean(cen * cen, axis=-1, keepdims=True) + 1e-06)
            mean_s[t, r, :] = mu
            rstd_s[t, r, :] = rstd
            act[place, r, :] = (cen * rstd * gains[t]).astype(BF)
            return 0

        lax.fori_loop(0, rows // step, body, 0)

    def project(t, wait_weights, dst):
        wait_weights.wait()
        place = jnp.where(c == t, 0, 2)
        for n in range(emb // 256):
            cols = slice(n * 256, (n + 1) * 256)
            unit[t, :, cols] = jnp.dot(
                act[place], weights[t, :, cols], preferred_element_type=F32
            )

        def body(i, _):
            r = pl.ds(pl.multiple_of(i * step, step), step)
            p = unit[t, r, :]
            inv = lax.rsqrt(jnp.sum(p * p, axis=-1, keepdims=True) + 1e-06)
            u = p * inv
            unit[t, r, :] = u
            inv_norm[t, r, :] = inv
            dst[r, :] = u.astype(BF)
            return 0

        lax.fori_loop(0, rows // step, body, 0)

    normalize(1, loads[0])
    project(1, loads[1], txts.at[2 + xh])
    pl.semaphore_wait(barrier, 16)

    own_text = txts.at[2 + xh]
    other_text = txts.at[2 + ox]
    t_copies = [
        remote(
            own_text,
            txts.at[xh],
            t_send.at[0],
            t_recv.at[xh],
            {"blk": ahead, "group": g},
        ),
        remote(own_text, txts.at[2 + xh], t_send.at[1], t_recv.at[2], partner),
    ]
    t_copies[1].start()
    t_copies[0].start()
    direct_text = remote(
        own_text,
        txts.at[xh],
        t_send.at[2],
        t_recv.at[xh],
        {"blk": ahead, "group": y * 2 + ox},
    )
    forward_text = remote(
        other_text,
        txts.at[ox],
        t_send.at[2],
        t_recv.at[ox],
        {"blk": ahead, "group": g},
    )

    @pl.when(c == 1)
    def _():
        direct_text.start()

    normalize(0, loads[2])
    project(0, loads[3], imgs.at[0])
    i_copies = [
        remote(
            imgs.at[0],
            imgs.at[d],
            i_send.at[d - 1],
            i_recv.at[d - 1],
            device_at(x, y + d, z, c),
        )
        for d in (1, 3, 2)
    ]
    for copy in i_copies:
        copy.start()
    a_copy = remote(act.at[2], act.at[1], a_sem.at[0], a_sem.at[1], other)
    a_copy.start()

    landed(other_text, t_recv.at[2])

    @pl.when(c == 0)
    def _():
        forward_text.start()

    a_copy.wait()
    for half in (0, 1):
        for n in range(width // 256):
            cols = slice(n * 256, (n + 1) * 256)
            act_t[cols, half * rows : (half + 1) * rows] = act[half, :, cols].T

    landed(txts.at[0], t_recv.at[0])
    landed(txts.at[1], t_recv.at[1])

    sharp = sharp_ref[0]
    off = off_ref[0]
    eye = (
        lax.broadcasted_iota(jnp.int32, (rows, rows), 0)
        == lax.broadcasted_iota(jnp.int32, (rows, rows), 1)
    ).astype(F32)

    def tile(s):
        img = imgs[s]
        for t in range(4):
            sim = lax.dot_general(img, txts[t], NT, preferred_element_type=F32)
            prob = jax.nn.sigmoid(sharp * sim + off)
            if s == 0 and t >= 2:
                prob = prob - eye * (xh == t - 2).astype(F32)
            coef[:, t * rows : (t + 1) * rows] = prob.astype(BF)
        for n in range(emb // 256):
            cols = slice(n * 256, (n + 1) * 256)
            d = jnp.dot(coef[:, 0:rows], txts[0, :, cols], preferred_element_type=F32)
            for t in range(1, 4):
                d += jnp.dot(
                    coef[:, t * rows : (t + 1) * rows],
                    txts[t, :, cols],
                    preferred_element_type=F32,
                )
            if s == 0:
                d_own[:, cols] = d
            else:
                di_send[s - 1, :, cols] = d.astype(BF)
        if s:
            di_copies[s - 1].start()
        for t in range(4):
            ct = coef[:, t * rows : (t + 1) * rows]
            part = lax.dot_general(ct, img, TN, preferred_element_type=F32)
            if s == 0:
                d_txt[t] = part
            else:
                d_txt[t] += part

    di_copies = [
        remote(
            di_send.at[s - 1],
            di_recv.at[s - 1],
            di_ss.at[s - 1],
            di_rs.at[s - 1],
            device_at(x, y + 4 - s, z, c),
        )
        for s in (1, 2, 3)
    ]
    tile(0)
    for s in (1, 3, 2):
        landed(imgs.at[s], i_recv.at[s - 1])
        tile(s)

    dt_copies = []
    for j in (0, 1):
        dt_send[j] = d_txt[j].astype(BF)
        dt_copies.append(
            remote(
                dt_send.at[j],
                dt_recv.at[jnp.where(c == 0, xh, j)],
                dt_ss.at[j],
                dt_rs.at[jnp.where(c == 0, xh, j)],
                {"blk": behind, "group": y * 2 + jnp.where(c == 0, j, xh)},
            )
        )
        dt_copies[j].start()
    dt_copies.append(
        remote(dt_send.at[2], dt_recv.at[2], dt_ss.at[2], dt_rs.at[2], partner)
    )

    @pl.when(c == 0)
    def _():
        landed(dt_recv.at[ox], dt_rs.at[ox])
        dt_send[2] = (d_txt[2 + ox] + dt_recv[ox].astype(F32)).astype(BF)
        dt_copies[2].start()

    @pl.when(c == 1)
    def _():
        dt_send[2] = d_txt[2 + ox].astype(BF)
        dt_copies[2].start()

    def head_backward(t, total):
        place = jnp.where(c == t, 0, 2)

        def body(i, _):
            r = pl.ds(pl.multiple_of(i * step, step), step)
            d = sharp * total(r)
            u = unit[t, r, :]
            dot = jnp.sum(u * d, axis=-1, keepdims=True)
            dp[place, r, :] = ((d - u * dot) * inv_norm[t, r, :]).astype(BF)
            return 0

        lax.fori_loop(0, rows // step, body, 0)

    def img_total(r):
        total = d_own[r, :]
        for s in range(3):
            total += di_recv[s, r, :].astype(F32)
        return total

    for s in range(3):
        landed(di_recv.at[s], di_rs.at[s])
    head_backward(0, img_total)
    dp_copy = remote(dp.at[2], dp.at[1], dp_sem.at[0], dp_sem.at[1], other)

    @pl.when(c == 1)
    def _():
        dp_copy.start()

    landed(dt_recv.at[2], dt_rs.at[2])
    landed(dt_recv.at[xh], dt_rs.at[xh])

    @pl.when(c == 1)
    def _():
        landed(dt_recv.at[ox], dt_rs.at[ox])

    first = jnp.where(c == 0, xh, 0)
    both = c.astype(F32)

    def txt_total(r):
        total = d_txt[2 + xh, r, :] + dt_recv[2, r, :].astype(F32)
        total += dt_recv[first, r, :].astype(F32)
        return total + both * dt_recv[1, r, :].astype(F32)

    head_backward(1, txt_total)

    @pl.when(c == 0)
    def _():
        dp_copy.start()

    landed(dp.at[1], dp_sem.at[1])

    def along_a(d):
        return device_at(
            jnp.where(c == 0, x, x + d), jnp.where(c == 0, y + d, y), z, c
        )

    def along_b(d):
        return device_at(
            jnp.where(c == 0, x + d, x), jnp.where(c == 0, y, y + d), z, c
        )

    pos_a = jnp.where(c == 0, y, x)
    pos_b = jnp.where(c == 0, x, y)

    for n in range(4):
        cols = slice(n * 256, (n + 1) * 256)
        part = jnp.dot(
            act_t[:, 0:rows], dp[0, :, cols], preferred_element_type=F32
        ) + jnp.dot(act_t[:, rows:], dp[1, :, cols], preferred_element_type=F32)
        part = part.astype(BF).reshape(8, 2, 96, 256)
        for xhi in range(2):
            for xlo in range(2):
                px = 2 * xhi + xlo
                wb[jnp.where(c == 0, n, px), jnp.where(c == 0, px, n)] = part[
                    :, xlo, :, xhi * 128 : (xhi + 1) * 128
                ]
    w1 = []
    for d in (2, 1, 3):
        w1.append(
            remote(
                wb.at[lax.rem(pos_a + d, 4)],
                wr1.at[d - 1],
                w1_ss.at[d - 1],
                w1_rs.at[d - 1],
                along_a(d),
            )
        )
        w1[-1].start()

    def features_backward(t, out):
        place = jnp.where(c == t, 0, 2)
        for n in range(width // 256):
            cols = slice(n * 256, (n + 1) * 256)
            d_act[:, cols] = lax.dot_general(
                dp[place], weights[t, cols, :], NT, preferred_element_type=F32
            )

        def body(i, _):
            r = pl.ds(pl.multiple_of(i * step, step), step)
            rstd = rstd_s[t, r, :]
            xhat = (feats[t, r, :].astype(F32) - mean_s[t, r, :]) * rstd
            ghat = d_act[r, :] * gains[t]
            m1 = jnp.mean(ghat, axis=-1, keepdims=True)
            m2 = jnp.mean(ghat * xhat, axis=-1, keepdims=True)
            out[r, :] = rstd * (ghat - m1 - xhat * m2)
            return 0

        lax.fori_loop(0, rows // step, body, 0)

    features_backward(0, gi_out)
    features_backward(1, gt_out)

    for d in (1, 2, 3):
        landed(wr1.at[d - 1], w1_rs.at[d - 1])
    for b in range(4):
        for zz in range(8):
            total = wb[pos_a, b, zz].astype(F32)
            for d in range(3):
                total += wr1[d, b, zz].astype(F32)
            s1[b, zz] = total.astype(BF)
    w2 = []
    for d in (2, 1, 3):
        w2.append(
            remote(
                s1.at[lax.rem(pos_b + d, 4)],
                wr2.at[d - 1],
                w2_ss.at[d - 1],
                w2_rs.at[d - 1],
                along_b(d),
            )
        )
        w2[-1].start()
    for d in (1, 2, 3):
        landed(wr2.at[d - 1], w2_rs.at[d - 1])
    for zz in range(8):
        total = s1[pos_b, zz].astype(F32)
        for d in range(3):
            total += wr2[d, zz].astype(F32)
        s2[zz] = total.astype(BF)
    w3 = []
    for d in (4, 3, 5, 2, 6, 1, 7):
        w3.append(
            remote(
                s2.at[lax.rem(z + d, 8)],
                wr3.at[d - 1],
                w3_ss.at[d - 1],
                w3_rs.at[d - 1],
                device_at(x, y, z + d, c),
            )
        )
        w3[-1].start()
    for d in range(1, 8):
        landed(wr3.at[d - 1], w3_rs.at[d - 1])
    total = s2[z].astype(F32)
    for d in range(7):
        total += wr3[d].astype(F32)
    total = (total * scale).reshape(2, 48, 128)
    fin[2] = total[0]
    fin[3] = total[1]
    f_copy = remote(fin.at[2 + oc], fin.at[c], f_sem.at[0], f_sem.at[1], other)
    f_copy.start()
    landed(fin.at[oc], f_sem.at[1])
    mine = fin[2 + c]
    theirs = fin[oc]
    wi_out[...] = jnp.where(c == 0, mine, theirs)
    wt_out[...] = jnp.where(c == 0, theirs, mine)

    for copy in t_copies + [direct_text] + i_copies + di_copies + dt_copies:
        copy.wait_send()
    for copy in w1 + w2 + w3 + [dp_copy, f_copy]:
        copy.wait_send()


def on_device(feat_i, feat_t, gain_i, gain_t, w_i, w_t, sharp, off):
    rows, width = feat_i.shape
    emb = w_i.shape[1]
    batch = rows * lax.axis_size("group") * lax.axis_size("blk")
    scale = math.sqrt(emb / batch)
    vmem = pl.BlockSpec(memory_space=pltpu.VMEM)
    smem = pl.BlockSpec(memory_space=pltpu.SMEM)
    hbm = pl.BlockSpec(memory_space=pl.ANY)
    dma = pltpu.SemaphoreType.DMA
    return pl.pallas_call(
        functools.partial(kernel, scale),
        name="siglip_grads",
        out_shape=(
            jax.ShapeDtypeStruct((rows, width), F32),
            jax.ShapeDtypeStruct((rows, width), F32),
            jax.ShapeDtypeStruct((48, 128), F32),
            jax.ShapeDtypeStruct((48, 128), F32),
        ),
        in_specs=[smem, smem, vmem, vmem, hbm, hbm, hbm, hbm],
        out_specs=(vmem, vmem, vmem, vmem),
        scratch_shapes=[
            pltpu.VMEM((2, rows, width), BF),
            pltpu.VMEM((2, width, emb), BF),
            pltpu.VMEM((2, 1, width), F32),
            pltpu.VMEM((3, rows, width), BF),
            pltpu.VMEM((width, 2 * rows), BF),
            pltpu.VMEM((2, rows, emb), F32),
            pltpu.VMEM((2, rows, 1), F32),
            pltpu.VMEM((2, rows, 1), F32),
            pltpu.VMEM((2, rows, 1), F32),
            pltpu.VMEM((4, rows, emb), BF),
            pltpu.VMEM((4, rows, emb), BF),
            pltpu.VMEM((rows, 4 * rows), BF),
            pltpu.VMEM((rows, emb), F32),
            pltpu.VMEM((4, rows, emb), F32),
            pltpu.VMEM((3, rows, emb), BF),
            pltpu.VMEM((3, rows, emb), BF),
            pltpu.VMEM((3, rows, emb), BF),
            pltpu.VMEM((3, rows, emb), BF),
            pltpu.VMEM((3, rows, emb), BF),
            pltpu.VMEM((rows, width), F32),
            pltpu.VMEM((4, 4, 8, 96, 128), BF),
            pltpu.VMEM((3, 4, 8, 96, 128), BF),
            pltpu.VMEM((4, 8, 96, 128), BF),
            pltpu.VMEM((3, 8, 96, 128), BF),
            pltpu.VMEM((8, 96, 128), BF),
            pltpu.VMEM((7, 96, 128), BF),
            pltpu.VMEM((4, 48, 128), F32),
            dma((4,)),
            dma((3,)),
            dma((3,)),
            dma((3,)),
            dma((3,)),
            dma((2,)),
            dma((3,)),
            dma((3,)),
            dma((3,)),
            dma((3,)),
            dma((2,)),
            dma((3,)),
            dma((3,)),
            dma((3,)),
            dma((3,)),
            dma((7,)),
            dma((7,)),
            dma((2,)),
        ],
        compiler_params=pltpu.CompilerParams(
            collective_id=0, has_side_effects=True, vmem_limit_bytes=60 << 20
        ),
        cost_estimate=pl.CostEstimate(
            flops=11 * 10**9, bytes_accessed=11 * 10**6, transcendentals=10**6
        ),
    )(
        sharp,
        off,
        gain_i.reshape(1, width),
        gain_t.reshape(1, width),
        feat_i,
        feat_t,
        w_i,
        w_t,
    )


def solution(mesh):
    rows = P(("blk", "group"), None)
    return jax.shard_map(
        on_device,
        mesh=mesh,
        in_specs=(rows, rows, P(), P(), P(), P(), P(), P()),
        out_specs=(rows, rows, P("blk", "group"), P("blk", "group")),
        check_vma=False,
    )
```

```python
import functools
import math

import jax
import jax.numpy as jnp
from jax import lax
from jax.experimental import pallas as pl
from jax.experimental.pallas import tpu as pltpu
from jax.sharding import PartitionSpec as P

BF = jnp.bfloat16
F32 = jnp.float32
NT = (((1,), (1,)), ((), ()))
TN = (((0,), (0,)), ((), ()))


def device_at(x, y, z, c):
    x, y, z = lax.rem(x, 4), lax.rem(y, 4), lax.rem(z, 8)
    return {"blk": z * 4 + lax.rem(x, 2) * 2 + c, "group": y * 2 + x // 2}


def remote(src, dst, send, recv, device):
    return pltpu.make_async_remote_copy(
        src_ref=src,
        dst_ref=dst,
        send_sem=send,
        recv_sem=recv,
        device_id=device,
        device_id_type=pl.DeviceIdType.MESH,
    )


def landed(ref, sem):
    pltpu.make_async_copy(ref, ref, sem).wait()


def kernel(
    scale,
    sharp_ref,
    off_ref,
    gain_i,
    gain_t,
    feat_i,
    feat_t,
    w_i,
    w_t,
    gi_out,
    gt_out,
    wi_out,
    wt_out,
    feats,
    weights,
    gains,
    act,
    act_t,
    unit,
    inv_norm,
    mean_s,
    rstd_s,
    imgs,
    txts,
    coef,
    d_own,
    d_txt,
    di_send,
    di_recv,
    di_pass,
    dt_send,
    dt_recv,
    dp,
    d_act,
    wb,
    w_pass,
    wr1,
    s1,
    wr2,
    s2,
    wr3,
    load_sem,
    i_send,
    i_recv,
    t_send,
    t_recv,
    a_sem,
    di_ss,
    di_rs,
    dt_ss,
    dt_rs,
    dp_sem,
    w1_ss,
    w1_rs,
    w2_ss,
    w2_rs,
    w3_ss,
    w3_rs,
):
    k = lax.axis_index("blk")
    g = lax.axis_index("group")
    c = lax.rem(k, 2)
    z = k // 4
    xl = lax.rem(k // 2, 2)
    y = g // 2
    xh = lax.rem(g, 2)
    x = 2 * xh + xl
    oc = 1 - c
    ox = 1 - xh
    other = {"blk": k + 1 - 2 * c, "group": g}
    partner = {"blk": k, "group": y * 2 + ox}
    behind = lax.rem(k + 31, 32)
    ahead = lax.rem(k + 1, 32)
    linked = lax.rem(k + 31 + 2 * c, 32)
    rows, width = feats.shape[1], feats.shape[2]
    emb = imgs.shape[2]

    loads = [
        pltpu.make_async_copy(feat_t, feats.at[1], load_sem.at[0]),
        pltpu.make_async_copy(w_t, weights.at[1], load_sem.at[1]),
        pltpu.make_async_copy(feat_i, feats.at[0], load_sem.at[2]),
        pltpu.make_async_copy(w_i, weights.at[0], load_sem.at[3]),
    ]
    for load in loads:
        load.start()

    barrier = pltpu.get_barrier_semaphore()
    partners = [device_at(x, y + d, z, c) for d in (1, 2, 3)]
    partners += [device_at(x + d, y, z, c) for d in (1, 2, 3)]
    partners += [device_at(x, y, z + d, c) for d in range(1, 8)]
    partners += [device_at(x, y, z + d, oc) for d in range(8)]
    partners += [{"blk": linked, "group": y * 2 + j} for j in (0, 1)]
    for device in partners:
        pl.semaphore_signal(
            barrier, inc=1, device_id=device, device_id_type=pl.DeviceIdType.MESH
        )
    gains[0] = gain_i[...].reshape(1, width)
    gains[1] = gain_t[...].reshape(1, width)

    step = 32

    def normalize(t, wait_features):
        wait_features.wait()
        place = jnp.where(c == t, 0, 2)

        def body(i, _):
            r = pl.ds(pl.multiple_of(i * step, step), step)
            v = feats[t, r, :].astype(F32)
            mu = jnp.mean(v, axis=-1, keepdims=True)
            cen = v - mu
            rstd = lax.rsqrt(jnp.mean(cen * cen, axis=-1, keepdims=True) + 1e-06)
            mean_s[t, r, :] = mu
            rstd_s[t, r, :] = rstd
            act[place, r, :] = (cen * rstd * gains[t]).astype(BF)
            return 0

        lax.fori_loop(0, rows // step, body, 0)

    def project(t, wait_weights, dst):
        wait_weights.wait()
        place = jnp.where(c == t, 0, 2)
        for n in range(emb // 256):
            cols = slice(n * 256, (n + 1) * 256)
            unit[t, :, cols] = jnp.dot(
                act[place], weights[t, :, cols], preferred_element_type=F32
            )

        def body(i, _):
            r = pl.ds(pl.multiple_of(i * step, step), step)
            p = unit[t, r, :]
            inv = lax.rsqrt(jnp.sum(p * p, axis=-1, keepdims=True) + 1e-06)
            u = p * inv
            unit[t, r, :] = u
            inv_norm[t, r, :] = inv
            dst[r, :] = u.astype(BF)
            return 0

        lax.fori_loop(0, rows // step, body, 0)

    normalize(1, loads[0])
    project(1, loads[1], txts.at[2 + xh])
    pl.semaphore_wait(barrier, 23)

    own_text = txts.at[2 + xh]
    other_text = txts.at[2 + ox]
    t_copies = [
        remote(
            own_text,
            txts.at[xh],
            t_send.at[0],
            t_recv.at[xh],
            {"blk": ahead, "group": g},
        ),
        remote(own_text, txts.at[2 + xh], t_send.at[1], t_recv.at[2], partner),
    ]
    t_copies[0].start()
    direct_text = remote(
        own_text,
        txts.at[xh],
        t_send.at[2],
        t_recv.at[xh],
        {"blk": ahead, "group": y * 2 + ox},
    )
    forward_text = remote(
        other_text,
        txts.at[ox],
        t_send.at[2],
        t_recv.at[ox],
        {"blk": ahead, "group": g},
    )

    @pl.when(c == 1)
    def _():
        direct_text.start()

    t_copies[1].start()
    normalize(0, loads[2])
    project(0, loads[3], imgs.at[0])
    half_a, half_b = pl.ds(0, rows // 2), pl.ds(rows // 2, rows // 2)
    up, down = device_at(x, y + 1, z, c), device_at(x, y + 3, z, c)
    i_copies = [
        remote(
            imgs.at[src, part], imgs.at[dst, part], i_send.at[n], i_recv.at[n], device
        )
        for n, (src, dst, part, device) in enumerate(
            (
                (0, 1, half_a, up),
                (0, 1, half_b, up),
                (0, 3, half_b, down),
                (0, 3, half_a, down),
                (1, 2, half_a, up),
                (3, 2, half_b, down),
            )
        )
    ]
    for n in (0, 2, 1, 3):
        i_copies[n].start()
    a_copy = remote(act.at[2], act.at[1], a_sem.at[0], a_sem.at[1], other)
    a_copy.start()

    sharp = sharp_ref[0]
    off = off_ref[0]
    own, late = 2 + xh, 2 + ox

    def pair(s, t, matching=False, fresh=False):
        img = imgs[s]
        sim = lax.dot_general(img, txts[t], NT, preferred_element_type=F32)
        prob = jax.nn.sigmoid(sharp * sim + off)
        if matching:
            row = lax.broadcasted_iota(jnp.int32, (rows, rows), 0)
            col = lax.broadcasted_iota(jnp.int32, (rows, rows), 1)
            prob = prob - (row == col).astype(F32)
        chosen = prob.astype(BF)
        coef[s, t] = chosen
        part = lax.dot_general(chosen, img, TN, preferred_element_type=F32)
        if fresh:
            d_txt[t] = part
        else:
            d_txt[t] += part

    def image_terms(s, dst):
        for n in range(emb // 256):
            cols = slice(n * 256, (n + 1) * 256)
            d = jnp.dot(coef[s, 0], txts[0, :, cols], preferred_element_type=F32)
            for t in range(1, 4):
                d += jnp.dot(coef[s, t], txts[t, :, cols], preferred_element_type=F32)
            dst[:, cols] = d.astype(dst.dtype)

    quarters = [pl.ds(n * rows // 4, rows // 4) for n in range(4)]
    di_copies = [
        remote(src, dst, di_ss.at[n], di_rs.at[n], device)
        for n, (src, dst, device) in enumerate(
            (
                (di_send.at[2, half_b], di_recv.at[0, half_b], up),
                (di_send.at[1, quarters[0]], di_pass.at[quarters[0]], up),
                (di_send.at[1, quarters[1]], di_pass.at[quarters[1]], up),
                (di_send.at[2, quarters[0]], di_recv.at[0, quarters[0]], up),
                (di_send.at[2, quarters[1]], di_recv.at[0, quarters[1]], up),
                (di_send.at[0, half_a], di_recv.at[1, half_a], down),
                (di_send.at[1, quarters[2]], di_pass.at[quarters[2]], down),
                (di_send.at[1, quarters[3]], di_pass.at[quarters[3]], down),
                (di_send.at[0, quarters[2]], di_recv.at[1, quarters[2]], down),
                (di_send.at[0, quarters[3]], di_recv.at[1, quarters[3]], down),
            )
        )
    ]
    dt_copies = []
    for j in (0, 1):
        dt_copies.append(
            remote(
                dt_send.at[j],
                dt_recv.at[jnp.where(c == 0, xh, j)],
                dt_ss.at[j],
                dt_rs.at[jnp.where(c == 0, xh, j)],
                {"blk": behind, "group": y * 2 + jnp.where(c == 0, j, xh)},
            )
        )
    dt_copies.append(
        remote(dt_send.at[2], dt_recv.at[2], dt_ss.at[2], dt_rs.at[2], partner)
    )

    pair(0, own, matching=True, fresh=True)
    a_copy.wait()
    for half in (0, 1):
        for n in range(width // 256):
            cols = slice(n * 256, (n + 1) * 256)
            act_t[cols, half * rows : (half + 1) * rows] = act[half, :, cols].T
    landed(txts.at[xh], t_recv.at[xh])
    pair(0, xh, fresh=True)
    i_copies[0].wait_recv()
    i_copies[4].start()
    i_copies[2].wait_recv()
    i_copies[5].start()

    @pl.when(c == 0)
    def _():
        landed(txts.at[ox], t_recv.at[ox])
        pair(0, ox, fresh=True)

    i_copies[1].wait_recv()
    i_copies[3].wait_recv()
    for s in (3, 1):
        pair(s, own)
        pair(s, xh)

    @pl.when(c == 0)
    def _():
        pair(3, ox)
        pair(1, ox)

    landed(other_text, t_recv.at[2])

    @pl.when(c == 0)
    def _():
        forward_text.start()

    @pl.when(c == 1)
    def _():
        landed(txts.at[ox], t_recv.at[ox])
        pair(0, ox, fresh=True)
        pair(3, ox)
        pair(1, ox)

    pair(3, late, fresh=True)
    image_terms(3, di_send.at[2])
    di_copies[0].start()
    pair(1, late)
    image_terms(1, di_send.at[0])
    di_copies[5].start()
    i_copies[4].wait_recv()
    i_copies[5].wait_recv()
    pair(2, xh)
    pair(2, ox)
    for j in (0, 1):
        dt_send[j] = d_txt[j].astype(BF)
        dt_copies[j].start()
    pair(2, late)
    pair(2, own)
    image_terms(2, di_send.at[1])
    for n in (1, 6, 2, 7):
        di_copies[n].start()
    pair(0, late)

    @pl.when(c == 0)
    def _():
        landed(dt_recv.at[ox], dt_rs.at[ox])
        dt_send[2] = (d_txt[2 + ox] + dt_recv[ox].astype(F32)).astype(BF)
        dt_copies[2].start()

    @pl.when(c == 1)
    def _():
        dt_send[2] = d_txt[2 + ox].astype(BF)
        dt_copies[2].start()

    def head_backward(t, total):
        place = jnp.where(c == t, 0, 2)

        def body(i, _):
            r = pl.ds(pl.multiple_of(i * step, step), step)
            d = sharp * total(r)
            u = unit[t, r, :]
            dot = jnp.sum(u * d, axis=-1, keepdims=True)
            dp[place, r, :] = ((d - u * dot) * inv_norm[t, r, :]).astype(BF)
            return 0

        lax.fori_loop(0, rows // step, body, 0)

    def img_total(r):
        total = d_own[r, :]
        for n in range(2):
            total += di_recv[n, r, :].astype(F32)
        return total

    image_terms(0, d_own)
    for n, slot in ((0, 2), (2, 0), (1, 2), (3, 0)):
        arrived, onward = ((1, 3), (2, 4), (6, 8), (7, 9))[n]
        di_copies[arrived].wait_recv()
        di_send[slot, quarters[n], :] = (
            di_send[slot, quarters[n], :].astype(F32)
            + di_pass[quarters[n], :].astype(F32)
        ).astype(BF)
        di_copies[onward].start()
    for n in (0, 5, 3, 8, 4, 9):
        di_copies[n].wait_recv()
    head_backward(0, img_total)
    dp_copy = remote(dp.at[2], dp.at[1], dp_sem.at[0], dp_sem.at[1], other)

    @pl.when(c == 1)
    def _():
        dp_copy.start()

    landed(dt_recv.at[2], dt_rs.at[2])
    landed(dt_recv.at[xh], dt_rs.at[xh])

    @pl.when(c == 1)
    def _():
        landed(dt_recv.at[ox], dt_rs.at[ox])

    first = jnp.where(c == 0, xh, 0)
    both = c.astype(F32)

    def txt_total(r):
        total = d_txt[2 + xh, r, :] + dt_recv[2, r, :].astype(F32)
        total += dt_recv[first, r, :].astype(F32)
        return total + both * dt_recv[1, r, :].astype(F32)

    head_backward(1, txt_total)

    @pl.when(c == 0)
    def _():
        dp_copy.start()

    landed(dp.at[1], dp_sem.at[1])

    def along_a(d):
        return device_at(
            jnp.where(c == 0, x, x + d), jnp.where(c == 0, y + d, y), z, c
        )

    pos_a = jnp.where(c == 0, y, x)
    pos_b = jnp.where(c == 0, x, y)
    fore, aft, far = (lax.rem(pos_a + d, 4) for d in (1, 3, 2))

    pieces = (
        [(wb.at[far, b], w_pass.at[b], along_a(1)) for b in (0, 1)]
        + [(wb.at[fore, b], wr1.at[0, b], along_a(1)) for b in (2, 3, 0, 1)]
        + [(wb.at[far, b], w_pass.at[b], along_a(3)) for b in (2, 3)]
        + [(wb.at[aft, b], wr1.at[1, b], along_a(3)) for b in (0, 1, 2, 3)]
    )
    w1 = [
        remote(src, dst, w1_ss.at[n], w1_rs.at[n], device)
        for n, (src, dst, device) in enumerate(pieces)
    ]

    for j in range(4):
        by_text = (0, 2, 1, 3)[j]
        n = jnp.where(c == 0, lax.rem(y + (2, 1, 3, 0)[j], 4), by_text)
        cols = pl.ds(pl.multiple_of(n * 256, 256), 256)
        part = jnp.dot(
            act_t[:, 0:rows], dp[0, :, cols], preferred_element_type=F32
        ) + jnp.dot(act_t[:, rows:], dp[1, :, cols], preferred_element_type=F32)
        part = part.astype(BF).reshape(8, 2, 2, 48, 256)
        for xhi in range(2):
            for xlo in range(2):
                px = 2 * xhi + xlo
                wb[jnp.where(c == 0, n, px), jnp.where(c == 0, px, n)] = part[
                    :, xlo, :, :, xhi * 128 : (xhi + 1) * 128
                ]

        @pl.when(c == 0)
        def _():
            for n in ((0, 6, 1, 7), (2, 3), (8, 9), ())[j]:
                w1[n].start()

        @pl.when(c == 1)
        def _():
            for n in ((0, 8), (6, 2), (1, 9), (7, 3))[j]:
                w1[n].start()

    def features_backward(t, out):
        place = jnp.where(c == t, 0, 2)
        for n in range(width // 256):
            cols = slice(n * 256, (n + 1) * 256)
            d_act[:, cols] = lax.dot_general(
                dp[place], weights[t, cols, :], NT, preferred_element_type=F32
            )

        def body(i, _):
            r = pl.ds(pl.multiple_of(i * step, step), step)
            rstd = rstd_s[t, r, :]
            xhat = (feats[t, r, :].astype(F32) - mean_s[t, r, :]) * rstd
            ghat = d_act[r, :] * gains[t]
            m1 = jnp.mean(ghat, axis=-1, keepdims=True)
            m2 = jnp.mean(ghat * xhat, axis=-1, keepdims=True)
            out[r, :] = rstd * (ghat - m1 - xhat * m2)
            return 0

        lax.fori_loop(0, rows // step, body, 0)

    features_backward(0, gi_out)
    for b, arrived, onward, chunk in (
        (0, 0, 4, fore),
        (2, 6, 10, aft),
        (1, 1, 5, fore),
        (3, 7, 11, aft),
    ):
        w1[arrived].wait_recv()
        for zz in range(8):
            wb[chunk, b, zz] = (
                wb[chunk, b, zz].astype(F32) + w_pass[b, zz].astype(F32)
            ).astype(BF)
        w1[onward].start()
    features_backward(1, gt_out)

    def w2_copy(b, slot, half, device):
        part = pl.ds(half * 4, 4)
        return remote(
            s1.at[b, part],
            wr2.at[slot, part],
            w2_ss.at[slot, half],
            w2_rs.at[slot, half],
            device,
        )

    for b, early, late_piece in ((0, 8, 4), (2, 2, 10), (1, 9, 5), (3, 3, 11)):
        w1[early].wait_recv()
        w1[late_piece].wait_recv()
        for zz in range(8):
            total = wb[pos_a, b, zz].astype(F32) + wr1[0, b, zz].astype(F32)
            s1[b, zz] = (total + wr1[1, b, zz].astype(F32)).astype(BF)

        @pl.when(pos_b != b)
        def _():
            for half in (0, 1):
                w2_copy(
                    b,
                    lax.rem(b + 3 - pos_b, 4),
                    half,
                    device_at(jnp.where(c == 0, b, x), jnp.where(c == 0, y, b), z, c),
                ).start()

    def w3_copy(zd, cd):
        return remote(
            s2.at[zd, cd],
            wr3.at[c, z],
            w3_ss.at[zd, cd],
            w3_rs.at[c, z],
            {"blk": zd * 4 + xl * 2 + cd, "group": g},
        )

    for half in (0, 1):
        for d in range(3):
            w2_copy(0, d, half, other).wait_recv()
        for zd in range(half * 4, half * 4 + 4):
            total = s1[pos_b, zd].astype(F32)
            for d in range(3):
                total += wr2[d, zd].astype(F32)
            s2[zd] = total.astype(BF)
            for cd in (0, 1):

                @pl.when((zd != z) | (cd != c))
                def _():
                    w3_copy(zd, cd).start()

    wr3[c, z] = s2[z, c]
    for t, out in ((0, wi_out), (1, wt_out)):
        for zs in range(8):

            @pl.when((zs != z) | (t != c))
            def _():
                landed(wr3.at[t, zs], w3_rs.at[t, zs])

        total = wr3[t, 0].astype(F32)
        for zs in range(1, 8):
            total += wr3[t, zs].astype(F32)
        out[...] = total * scale

    for copy in t_copies + [direct_text] + i_copies + di_copies + dt_copies:
        copy.wait_send()
    for copy in w1 + [dp_copy]:
        copy.wait_send()
    for half in (0, 1):
        for d in range(3):
            w2_copy(0, d, half, other).wait_send()
    for zd in range(8):
        for cd in (0, 1):

            @pl.when((zd != z) | (cd != c))
            def _():
                w3_copy(zd, cd).wait_send()


def hand_out(*refs):
    copies = [
        pltpu.make_async_copy(refs[n], refs[4 + n], refs[8].at[n]) for n in range(4)
    ]
    for copy in copies:
        copy.start()
    for copy in copies:
        copy.wait()


def on_device(feat_i, feat_t, gain_i, gain_t, w_i, w_t, sharp, off):
    rows, width = feat_i.shape
    emb = w_i.shape[1]
    batch = rows * lax.axis_size("group") * lax.axis_size("blk")
    scale = math.sqrt(emb / batch)
    vmem = pl.BlockSpec(memory_space=pltpu.VMEM)
    smem = pl.BlockSpec(memory_space=pltpu.SMEM)
    hbm = pl.BlockSpec(memory_space=pl.ANY)
    dma = pltpu.SemaphoreType.DMA
    grads = pl.pallas_call(
        functools.partial(kernel, scale),
        name="siglip_grads",
        out_shape=(
            pltpu.VMEM((rows, width), F32),
            pltpu.VMEM((rows, width), F32),
            pltpu.VMEM((48, 128), F32),
            pltpu.VMEM((48, 128), F32),
        ),
        in_specs=[smem, smem, vmem, vmem, hbm, hbm, hbm, hbm],
        out_specs=(vmem, vmem, vmem, vmem),
        scratch_shapes=[
            pltpu.VMEM((2, rows, width), BF),
            pltpu.VMEM((2, width, emb), BF),
            pltpu.VMEM((2, 1, width), F32),
            pltpu.VMEM((3, rows, width), BF),
            pltpu.VMEM((width, 2 * rows), BF),
            pltpu.VMEM((2, rows, emb), F32),
            pltpu.VMEM((2, rows, 1), F32),
            pltpu.VMEM((2, rows, 1), F32),
            pltpu.VMEM((2, rows, 1), F32),
            pltpu.VMEM((4, rows, emb), BF),
            pltpu.VMEM((4, rows, emb), BF),
            pltpu.VMEM((4, 4, rows, rows), BF),
            pltpu.VMEM((rows, emb), F32),
            pltpu.VMEM((4, rows, emb), F32),
            pltpu.VMEM((3, rows, emb), BF),
            pltpu.VMEM((2, rows, emb), BF),
            pltpu.VMEM((rows, emb), BF),
            pltpu.VMEM((3, rows, emb), BF),
            pltpu.VMEM((3, rows, emb), BF),
            pltpu.VMEM((3, rows, emb), BF),
            pltpu.VMEM((rows, width), F32),
            pltpu.VMEM((4, 4, 8, 2, 48, 128), BF),
            pltpu.VMEM((4, 8, 2, 48, 128), BF),
            pltpu.VMEM((2, 4, 8, 2, 48, 128), BF),
            pltpu.VMEM((4, 8, 2, 48, 128), BF),
            pltpu.VMEM((3, 8, 2, 48, 128), BF),
            pltpu.VMEM((8, 2, 48, 128), BF),
            pltpu.VMEM((2, 8, 48, 128), BF),
            dma((4,)),
            dma((6,)),
            dma((6,)),
            dma((3,)),
            dma((3,)),
            dma((2,)),
            dma((10,)),
            dma((10,)),
            dma((3,)),
            dma((3,)),
            dma((2,)),
            dma((12,)),
            dma((12,)),
            dma((3, 2)),
            dma((3, 2)),
            dma((8, 2)),
            dma((2, 8)),
        ],
        compiler_params=pltpu.CompilerParams(
            collective_id=0, has_side_effects=True, vmem_limit_bytes=54 << 20
        ),
        cost_estimate=pl.CostEstimate(
            flops=11 * 10**9, bytes_accessed=11 * 10**6, transcendentals=10**6
        ),
    )(
        sharp,
        off,
        gain_i,
        gain_t,
        feat_i,
        feat_t,
        w_i,
        w_t,
    )
    return pl.pallas_call(
        hand_out,
        name="hand_out",
        out_shape=tuple(jax.ShapeDtypeStruct(a.shape, a.dtype) for a in grads),
        in_specs=[hbm] * 4,
        out_specs=(hbm,) * 4,
        scratch_shapes=[dma((4,))],
        compiler_params=pltpu.CompilerParams(vmem_limit_bytes=1 << 20),
    )(*grads)


def solution(mesh):
    rows = P(("blk", "group"), None)
    return jax.shard_map(
        on_device,
        mesh=mesh,
        in_specs=(rows, rows, P(), P(), P(), P(), P(), P()),
        out_specs=(rows, rows, P("blk", "group"), P("blk", "group")),
        check_vma=False,
    )
```

```python
import functools
import math

import jax
import jax.numpy as jnp
from jax import lax
from jax.experimental import pallas as pl
from jax.experimental.pallas import tpu as pltpu
from jax.sharding import PartitionSpec as P

BF = jnp.bfloat16
UNROLL = 8
F32 = jnp.float32
NT = (((1,), (1,)), ((), ()))
TN = (((0,), (0,)), ((), ()))


def device_at(x, y, z, c):
    x, y, z = lax.rem(x, 4), lax.rem(y, 4), lax.rem(z, 8)
    return {"blk": z * 4 + lax.rem(x, 2) * 2 + c, "group": y * 2 + x // 2}


def remote(src, dst, send, recv, device):
    return pltpu.make_async_remote_copy(
        src_ref=src,
        dst_ref=dst,
        send_sem=send,
        recv_sem=recv,
        device_id=device,
        device_id_type=pl.DeviceIdType.MESH,
    )


def landed(ref, sem):
    pltpu.make_async_copy(ref, ref, sem).wait()


def kernel(
    scale,
    sharp_hbm,
    off_hbm,
    gain_i,
    gain_t,
    feat_i,
    feat_t,
    w_i,
    w_t,
    gi_out,
    gt_out,
    wi_out,
    wt_out,
    sharp_ref,
    off_ref,
    gain_v,
    small_sem,
    feats,
    weights,
    gains,
    act,
    act_t,
    unit,
    inv_norm,
    mean_s,
    rstd_s,
    imgs,
    txts,
    coef,
    d_own,
    d_txt,
    di_send,
    di_recv,
    di_pass,
    dt_send,
    dt_recv,
    dp,
    d_act,
    wb,
    w_pass,
    wr1,
    s1,
    wr2,
    s2,
    wr3,
    load_sem,
    i_send,
    i_recv,
    t_send,
    t_recv,
    a_sem,
    di_ss,
    di_rs,
    dt_ss,
    dt_rs,
    dp_ss,
    dp_rs,
    w1_ss,
    w1_rs,
    w2_ss,
    w2_rs,
    w3_ss,
    w3_rs,
):
    k = lax.axis_index("blk")
    g = lax.axis_index("group")
    c = lax.rem(k, 2)
    z = k // 4
    xl = lax.rem(k // 2, 2)
    y = g // 2
    xh = lax.rem(g, 2)
    x = 2 * xh + xl
    oc = 1 - c
    ox = 1 - xh
    other = {"blk": k + 1 - 2 * c, "group": g}
    partner = {"blk": k, "group": y * 2 + ox}
    behind = lax.rem(k + 31, 32)
    ahead = lax.rem(k + 1, 32)
    linked = lax.rem(k + 31 + 2 * c, 32)
    rows, width = feats.shape[1], feats.shape[2]
    emb = imgs.shape[2]

    small = [
        pltpu.make_async_copy(src, dst, small_sem.at[n])
        for n, (src, dst) in enumerate(
            (
                (gain_t, gain_v.at[1]),
                (gain_i, gain_v.at[0]),
                (sharp_hbm, sharp_ref),
                (off_hbm, off_ref),
            )
        )
    ]
    for load in small:
        load.start()
    loads = [
        pltpu.make_async_copy(feat_t, feats.at[1], load_sem.at[0]),
        pltpu.make_async_copy(w_t, weights.at[1], load_sem.at[1]),
        pltpu.make_async_copy(feat_i, feats.at[0], load_sem.at[2]),
        pltpu.make_async_copy(w_i, weights.at[0], load_sem.at[3]),
    ]
    for n in (0, 2, 1, 3):
        loads[n].start()

    barrier = pltpu.get_barrier_semaphore()
    partners = [device_at(x, y + d, z, c) for d in (1, 2, 3)]
    partners += [device_at(x + d, y, z, c) for d in (1, 2, 3)]
    partners += [device_at(x, y, z + d, c) for d in range(1, 8)]
    partners += [device_at(x, y, z + d, oc) for d in range(8)]
    partners += [{"blk": linked, "group": y * 2 + j} for j in (0, 1)]
    for device in partners:
        pl.semaphore_signal(
            barrier, inc=1, device_id=device, device_id_type=pl.DeviceIdType.MESH
        )
    for load in small:
        load.wait()
    gains[0] = gain_v[0].reshape(1, width)
    gains[1] = gain_v[1].reshape(1, width)

    step = 32

    def normalize(t, wait_features):
        wait_features.wait()
        place = jnp.where(c == t, 0, 2)

        def body(i, _):
            r = pl.ds(pl.multiple_of(i * step, step), step)
            v = feats[t, r, :].astype(F32)
            mu = jnp.mean(v, axis=-1, keepdims=True)
            cen = v - mu
            rstd = lax.rsqrt(jnp.mean(cen * cen, axis=-1, keepdims=True) + 1e-06)
            mean_s[t, r, :] = mu
            rstd_s[t, r, :] = rstd
            act[place, r, :] = (cen * rstd * gains[t]).astype(BF)
            return 0

        lax.fori_loop(0, rows // step, body, 0, unroll=UNROLL)

    def project(t, wait_weights, dst):
        wait_weights.wait()
        place = jnp.where(c == t, 0, 2)
        for n in range(emb // 256):
            cols = slice(n * 256, (n + 1) * 256)
            unit[t, :, cols] = jnp.dot(
                act[place], weights[t, :, cols], preferred_element_type=F32
            )

        def body(i, _):
            r = pl.ds(pl.multiple_of(i * step, step), step)
            p = unit[t, r, :]
            inv = lax.rsqrt(jnp.sum(p * p, axis=-1, keepdims=True) + 1e-06)
            u = p * inv
            unit[t, r, :] = u
            inv_norm[t, r, :] = inv
            dst[r, :] = u.astype(BF)
            return 0

        lax.fori_loop(0, rows // step, body, 0, unroll=UNROLL)

    normalize(1, loads[0])
    normalize(0, loads[2])
    project(1, loads[1], txts.at[2 + xh])
    pl.semaphore_wait(barrier, 23)

    own_text = txts.at[2 + xh]
    other_text = txts.at[2 + ox]
    t_copies = [
        remote(
            own_text,
            txts.at[xh],
            t_send.at[0],
            t_recv.at[xh],
            {"blk": ahead, "group": g},
        ),
        remote(own_text, txts.at[2 + xh], t_send.at[1], t_recv.at[2], partner),
    ]
    t_copies[0].start()
    direct_text = remote(
        own_text,
        txts.at[xh],
        t_send.at[2],
        t_recv.at[xh],
        {"blk": ahead, "group": y * 2 + ox},
    )
    forward_text = remote(
        other_text,
        txts.at[ox],
        t_send.at[2],
        t_recv.at[ox],
        {"blk": ahead, "group": g},
    )

    @pl.when(c == 1)
    def _():
        direct_text.start()

    t_copies[1].start()
    project(0, loads[3], imgs.at[0])
    half_a, half_b = pl.ds(0, rows // 2), pl.ds(rows // 2, rows // 2)
    up, down = device_at(x, y + 1, z, c), device_at(x, y + 3, z, c)
    i_copies = [
        remote(
            imgs.at[src, part], imgs.at[dst, part], i_send.at[n], i_recv.at[n], device
        )
        for n, (src, dst, part, device) in enumerate(
            (
                (0, 1, half_a, up),
                (0, 1, half_b, up),
                (0, 3, half_b, down),
                (0, 3, half_a, down),
                (1, 2, half_a, up),
                (3, 2, half_b, down),
            )
        )
    ]
    for n in (0, 2, 1, 3):
        i_copies[n].start()
    a_copy = remote(act.at[2], act.at[1], a_sem.at[0], a_sem.at[1], other)
    a_copy.start()

    sharp = sharp_ref[0]
    off = off_ref[0]
    own, late = 2 + xh, 2 + ox

    def pairs(*todo, matching=False):
        for s, t in todo:
            sim = lax.dot_general(imgs[s], txts[t], NT, preferred_element_type=F32)
            prob = jax.nn.sigmoid(sharp * sim + off)
            if matching:
                row = lax.broadcasted_iota(jnp.int32, (rows, rows), 0)
                col = lax.broadcasted_iota(jnp.int32, (rows, rows), 1)
                prob = prob - (row == col).astype(F32)
            coef[s, t] = prob.astype(BF)

    def text_terms(t, shards):
        total = lax.dot_general(
            coef[shards[0], t], imgs[shards[0]], TN, preferred_element_type=F32
        )
        for s in shards[1:]:
            total += lax.dot_general(
                coef[s, t], imgs[s], TN, preferred_element_type=F32
            )
        return total

    def image_terms(s, dst):
        for n in range(emb // 256):
            cols = slice(n * 256, (n + 1) * 256)
            d = jnp.dot(coef[s, 0], txts[0, :, cols], preferred_element_type=F32)
            for t in range(1, 4):
                d += jnp.dot(coef[s, t], txts[t, :, cols], preferred_element_type=F32)
            dst[:, cols] = d.astype(dst.dtype)

    quarters = [pl.ds(n * rows // 4, rows // 4) for n in range(4)]
    di_copies = [
        remote(src, dst, di_ss.at[n], di_rs.at[n], device)
        for n, (src, dst, device) in enumerate(
            (
                (di_send.at[2, half_b], di_recv.at[0, half_b], up),
                (di_send.at[1, quarters[0]], di_pass.at[quarters[0]], up),
                (di_send.at[1, quarters[1]], di_pass.at[quarters[1]], up),
                (di_send.at[2, quarters[0]], di_recv.at[0, quarters[0]], up),
                (di_send.at[2, quarters[1]], di_recv.at[0, quarters[1]], up),
                (di_send.at[0, half_a], di_recv.at[1, half_a], down),
                (di_send.at[1, quarters[2]], di_pass.at[quarters[2]], down),
                (di_send.at[1, quarters[3]], di_pass.at[quarters[3]], down),
                (di_send.at[0, quarters[2]], di_recv.at[1, quarters[2]], down),
                (di_send.at[0, quarters[3]], di_recv.at[1, quarters[3]], down),
            )
        )
    ]
    dt_copies = []
    for j in (0, 1):
        dt_copies.append(
            remote(
                dt_send.at[j],
                dt_recv.at[jnp.where(c == 0, xh, j)],
                dt_ss.at[j],
                dt_rs.at[jnp.where(c == 0, xh, j)],
                {"blk": behind, "group": y * 2 + jnp.where(c == 0, j, xh)},
            )
        )
    dt_copies.append(
        remote(dt_send.at[2], dt_recv.at[2], dt_ss.at[2], dt_rs.at[2], partner)
    )

    pairs((0, own), matching=True)
    a_copy.wait()
    for half in (0, 1):
        for n in range(width // 256):
            cols = slice(n * 256, (n + 1) * 256)
            act_t[cols, half * rows : (half + 1) * rows] = act[half, :, cols].T
    i_copies[0].wait_recv()
    i_copies[4].start()
    i_copies[2].wait_recv()
    i_copies[5].start()

    @pl.when(c == 0)
    def _():
        landed(other_text, t_recv.at[2])
        forward_text.start()

    landed(txts.at[xh], t_recv.at[xh])
    pairs((0, xh))
    i_copies[1].wait_recv()
    i_copies[3].wait_recv()
    pairs((3, own), (1, own), (3, xh), (1, xh))
    d_txt[xh] = text_terms(xh, (0, 1, 3))
    landed(txts.at[ox], t_recv.at[ox])
    pairs((0, ox), (3, ox), (1, ox))
    d_txt[ox] = text_terms(ox, (0, 1, 3))

    @pl.when(c == 1)
    def _():
        landed(other_text, t_recv.at[2])

    pairs((3, late), (1, late))
    image_terms(3, di_send.at[2])
    di_copies[0].start()
    image_terms(1, di_send.at[0])
    di_copies[5].start()
    i_copies[4].wait_recv()
    i_copies[5].wait_recv()
    pairs((2, xh), (2, ox))
    for j in (0, 1):
        dt_send[j] = (d_txt[j] + text_terms(j, (2,))).astype(BF)
        dt_copies[j].start()
    pairs((2, own), (2, late), (0, late))
    image_terms(2, di_send.at[1])
    for n in (1, 6, 2, 7):
        di_copies[n].start()
    d_txt[late] = text_terms(late, (0, 1, 2, 3))

    @pl.when(c == 0)
    def _():
        landed(dt_recv.at[ox], dt_rs.at[ox])
        dt_send[2] = (d_txt[2 + ox] + dt_recv[ox].astype(F32)).astype(BF)
        dt_copies[2].start()

    @pl.when(c == 1)
    def _():
        dt_send[2] = d_txt[2 + ox].astype(BF)
        dt_copies[2].start()

    def head_backward(t, total):
        place = jnp.where(c == t, 0, 2)

        def body(i, _):
            r = pl.ds(pl.multiple_of(i * step, step), step)
            d = sharp * total(r)
            u = unit[t, r, :]
            dot = jnp.sum(u * d, axis=-1, keepdims=True)
            at = pl.ds(pl.multiple_of(place * rows + i * step, step), step)
            dp[at, :] = ((d - u * dot) * inv_norm[t, r, :]).astype(BF)
            return 0

        lax.fori_loop(0, rows // step, body, 0, unroll=UNROLL)

    def img_total(r):
        total = d_own[r, :]
        for n in range(2):
            total += di_recv[n, r, :].astype(F32)
        return total

    d_txt[own] = text_terms(own, (0, 1, 2, 3))
    image_terms(0, d_own)
    for n, slot in ((0, 2), (2, 0), (1, 2), (3, 0)):
        arrived, onward = ((1, 3), (2, 4), (6, 8), (7, 9))[n]
        di_copies[arrived].wait_recv()
        di_send[slot, quarters[n], :] = (
            di_send[slot, quarters[n], :].astype(F32)
            + di_pass[quarters[n], :].astype(F32)
        ).astype(BF)
        di_copies[onward].start()
    for n in (0, 5, 3, 8, 4, 9):
        di_copies[n].wait_recv()
    head_backward(0, img_total)
    img_order = [lax.rem(y + d, 4) for d in (2, 1, 3, 0)]
    txt_order = (0, 2, 1, 3)

    def columns(j, core):
        n = jnp.where(core == 0, img_order[j], txt_order[j])
        return pl.ds(pl.multiple_of(n * 256, 256), 256)

    dp_copies = [
        remote(
            dp.at[pl.ds(2 * rows, rows), columns(j, oc)],
            dp.at[pl.ds(rows, rows), columns(j, oc)],
            dp_ss.at[j],
            dp_rs.at[j],
            other,
        )
        for j in range(4)
    ]

    @pl.when(c == 1)
    def _():
        for copy in dp_copies:
            copy.start()

    landed(dt_recv.at[2], dt_rs.at[2])
    landed(dt_recv.at[xh], dt_rs.at[xh])

    @pl.when(c == 1)
    def _():
        landed(dt_recv.at[ox], dt_rs.at[ox])

    first = jnp.where(c == 0, xh, 0)
    both = c.astype(F32)

    def txt_total(r):
        total = d_txt[2 + xh, r, :] + dt_recv[2, r, :].astype(F32)
        total += dt_recv[first, r, :].astype(F32)
        return total + both * dt_recv[1, r, :].astype(F32)

    head_backward(1, txt_total)

    @pl.when(c == 0)
    def _():
        for copy in dp_copies:
            copy.start()


    def along_a(d):
        return device_at(
            jnp.where(c == 0, x, x + d), jnp.where(c == 0, y + d, y), z, c
        )

    pos_a = jnp.where(c == 0, y, x)
    pos_b = jnp.where(c == 0, x, y)
    fore, aft, far = (lax.rem(pos_a + d, 4) for d in (1, 3, 2))

    pieces = (
        [(wb.at[far, b], w_pass.at[b], along_a(1)) for b in (0, 1)]
        + [(wb.at[fore, b], wr1.at[0, b], along_a(1)) for b in (2, 3, 0, 1)]
        + [(wb.at[far, b], w_pass.at[b], along_a(3)) for b in (2, 3)]
        + [(wb.at[aft, b], wr1.at[1, b], along_a(3)) for b in (0, 1, 2, 3)]
    )
    w1 = [
        remote(src, dst, w1_ss.at[n], w1_rs.at[n], device)
        for n, (src, dst, device) in enumerate(pieces)
    ]

    for j in range(4):
        n = jnp.where(c == 0, img_order[j], txt_order[j])
        cols = columns(j, c)
        landed(dp.at[pl.ds(rows, rows), cols], dp_rs.at[j])
        part = jnp.dot(
            act_t[...], dp[0 : 2 * rows, cols], preferred_element_type=F32
        )
        part = part.astype(BF).reshape(8, 2, 2, 48, 256)
        for xhi in range(2):
            for xlo in range(2):
                px = 2 * xhi + xlo
                wb[jnp.where(c == 0, n, px), jnp.where(c == 0, px, n)] = part[
                    :, xlo, :, :, xhi * 128 : (xhi + 1) * 128
                ]

        @pl.when(c == 0)
        def _():
            for n in ((0, 6, 1, 7), (2,), (8,), ())[j]:
                w1[n].start()

        @pl.when(c == 1)
        def _():
            for n in ((0, 8), (6, 2), (1,), (7,))[j]:
                w1[n].start()

    def features_backward(t, out):
        place = jnp.where(c == t, 0, 2)
        dproj = dp[pl.ds(pl.multiple_of(place * rows, rows), rows), :]
        for n in range(width // 256):
            cols = slice(n * 256, (n + 1) * 256)
            d_act[:, cols] = lax.dot_general(
                dproj, weights[t, cols, :], NT, preferred_element_type=F32
            )

        def body(i, _):
            r = pl.ds(pl.multiple_of(i * step, step), step)
            rstd = rstd_s[t, r, :]
            xhat = (feats[t, r, :].astype(F32) - mean_s[t, r, :]) * rstd
            ghat = d_act[r, :] * gains[t]
            m1 = jnp.mean(ghat, axis=-1, keepdims=True)
            m2 = jnp.mean(ghat * xhat, axis=-1, keepdims=True)
            out[r, :] = rstd * (ghat - m1 - xhat * m2)
            return 0

        lax.fori_loop(0, rows // step, body, 0, unroll=UNROLL)

    features_backward(0, gi_out)
    for b, arrived, onward, chunk in (
        (0, 0, 4, fore),
        (2, 6, 10, aft),
        (1, 1, 5, fore),
        (3, 7, 11, aft),
    ):
        w1[arrived].wait_recv()
        for zz in range(8):
            wb[chunk, b, zz] = (
                wb[chunk, b, zz].astype(F32) + w_pass[b, zz].astype(F32)
            ).astype(BF)
        w1[onward].start()
        if b == 2:
            w1[3].start()
            w1[9].start()
    features_backward(1, gt_out)

    def w2_copy(b, slot, half, device):
        part = pl.ds(half * 4, 4)
        return remote(
            s1.at[b, part],
            wr2.at[slot, part],
            w2_ss.at[slot, half],
            w2_rs.at[slot, half],
            device,
        )

    def w2_start(b, half):
        device = device_at(jnp.where(c == 0, b, x), jnp.where(c == 0, y, b), z, c)
        w2_copy(b, lax.rem(b + 3 - pos_b, 4), half, device).start()

    for b, early, late_piece in ((0, 8, 4), (2, 2, 10), (1, 9, 5), (3, 3, 11)):
        w1[early].wait_recv()
        w1[late_piece].wait_recv()
        for zz in range(8):
            total = wb[pos_a, b, zz].astype(F32) + wr1[0, b, zz].astype(F32)
            s1[b, zz] = (total + wr1[1, b, zz].astype(F32)).astype(BF)

        @pl.when(pos_b != b)
        def _():
            w2_start(b, 0)
            w2_start(b, 1)

    def w3_copy(zd, cd):
        return remote(
            s2.at[zd, cd],
            wr3.at[c, z],
            w3_ss.at[zd, cd],
            w3_rs.at[c, z],
            {"blk": zd * 4 + xl * 2 + cd, "group": g},
        )

    for half in (0, 1):
        for d in range(3):
            w2_copy(0, d, half, other).wait_recv()
        for zd in range(half * 4, half * 4 + 4):
            total = s1[pos_b, zd].astype(F32)
            for d in range(3):
                total += wr2[d, zd].astype(F32)
            s2[zd] = total.astype(BF)
            for cd in (0, 1):

                @pl.when((zd != z) | (cd != c))
                def _():
                    w3_copy(zd, cd).start()

    wr3[c, z] = s2[z, c]
    for t, out in ((0, wi_out), (1, wt_out)):
        for zs in range(8):

            @pl.when((zs != z) | (t != c))
            def _():
                landed(wr3.at[t, zs], w3_rs.at[t, zs])

        total = wr3[t, 0].astype(F32)
        for zs in range(1, 8):
            total += wr3[t, zs].astype(F32)
        out[...] = total * scale

    for copy in t_copies + [direct_text] + i_copies + di_copies + dt_copies:
        copy.wait_send()
    for copy in w1 + dp_copies:
        copy.wait_send()
    for half in (0, 1):
        for d in range(3):
            w2_copy(0, d, half, other).wait_send()
    for zd in range(8):
        for cd in (0, 1):

            @pl.when((zd != z) | (cd != c))
            def _():
                w3_copy(zd, cd).wait_send()


def hand_out(*refs):
    copies = [
        pltpu.make_async_copy(refs[n], refs[4 + n], refs[8].at[n]) for n in range(4)
    ]
    for copy in copies:
        copy.start()
    for copy in copies:
        copy.wait()


def on_device(feat_i, feat_t, gain_i, gain_t, w_i, w_t, sharp, off):
    rows, width = feat_i.shape
    emb = w_i.shape[1]
    batch = rows * lax.axis_size("group") * lax.axis_size("blk")
    scale = math.sqrt(emb / batch)
    vmem = pl.BlockSpec(memory_space=pltpu.VMEM)
    hbm = pl.BlockSpec(memory_space=pl.ANY)
    dma = pltpu.SemaphoreType.DMA
    grads = pl.pallas_call(
        functools.partial(kernel, scale),
        name="siglip_grads",
        out_shape=(
            pltpu.VMEM((rows, width), F32),
            pltpu.VMEM((rows, width), F32),
            pltpu.VMEM((48, 128), F32),
            pltpu.VMEM((48, 128), F32),
        ),
        in_specs=[hbm] * 8,
        out_specs=(vmem, vmem, vmem, vmem),
        scratch_shapes=[
            pltpu.SMEM((1,), F32),
            pltpu.SMEM((1,), F32),
            pltpu.VMEM((2, width), F32),
            dma((4,)),
            pltpu.VMEM((2, rows, width), BF),
            pltpu.VMEM((2, width, emb), BF),
            pltpu.VMEM((2, 1, width), F32),
            pltpu.VMEM((3, rows, width), BF),
            pltpu.VMEM((width, 2 * rows), BF),
            pltpu.VMEM((2, rows, emb), F32),
            pltpu.VMEM((2, rows, 1), F32),
            pltpu.VMEM((2, rows, 1), F32),
            pltpu.VMEM((2, rows, 1), F32),
            pltpu.VMEM((4, rows, emb), BF),
            pltpu.VMEM((4, rows, emb), BF),
            pltpu.VMEM((4, 4, rows, rows), BF),
            pltpu.VMEM((rows, emb), F32),
            pltpu.VMEM((4, rows, emb), F32),
            pltpu.VMEM((3, rows, emb), BF),
            pltpu.VMEM((2, rows, emb), BF),
            pltpu.VMEM((rows, emb), BF),
            pltpu.VMEM((3, rows, emb), BF),
            pltpu.VMEM((3, rows, emb), BF),
            pltpu.VMEM((3 * rows, emb), BF),
            pltpu.VMEM((rows, width), F32),
            pltpu.VMEM((4, 4, 8, 2, 48, 128), BF),
            pltpu.VMEM((4, 8, 2, 48, 128), BF),
            pltpu.VMEM((2, 4, 8, 2, 48, 128), BF),
            pltpu.VMEM((4, 8, 2, 48, 128), BF),
            pltpu.VMEM((3, 8, 2, 48, 128), BF),
            pltpu.VMEM((8, 2, 48, 128), BF),
            pltpu.VMEM((2, 8, 48, 128), BF),
            dma((4,)),
            dma((6,)),
            dma((6,)),
            dma((3,)),
            dma((3,)),
            dma((2,)),
            dma((10,)),
            dma((10,)),
            dma((3,)),
            dma((3,)),
            dma((4,)),
            dma((4,)),
            dma((12,)),
            dma((12,)),
            dma((3, 2)),
            dma((3, 2)),
            dma((8, 2)),
            dma((2, 8)),
        ],
        compiler_params=pltpu.CompilerParams(
            collective_id=0, has_side_effects=True, vmem_limit_bytes=54 << 20
        ),
        cost_estimate=pl.CostEstimate(
            flops=11 * 10**9, bytes_accessed=11 * 10**6, transcendentals=10**6
        ),
    )(
        sharp,
        off,
        gain_i,
        gain_t,
        feat_i,
        feat_t,
        w_i,
        w_t,
    )
    return pl.pallas_call(
        hand_out,
        name="hand_out",
        out_shape=tuple(jax.ShapeDtypeStruct(a.shape, a.dtype) for a in grads),
        in_specs=[hbm] * 4,
        out_specs=(hbm,) * 4,
        scratch_shapes=[dma((4,))],
        compiler_params=pltpu.CompilerParams(vmem_limit_bytes=1 << 20),
    )(*grads)


def solution(mesh):
    rows = P(("blk", "group"), None)
    return jax.shard_map(
        on_device,
        mesh=mesh,
        in_specs=(rows, rows, P(), P(), P(), P(), P(), P()),
        out_specs=(rows, rows, P("blk", "group"), P("blk", "group")),
        check_vma=False,
    )
```

```python
import functools
import math

import jax
import jax.numpy as jnp
from jax import lax
from jax.experimental import pallas as pl
from jax.experimental.pallas import tpu as pltpu
from jax.sharding import PartitionSpec as P

BF = jnp.bfloat16
UNROLL = 8
F32 = jnp.float32
NT = (((1,), (1,)), ((), ()))
TN = (((0,), (0,)), ((), ()))


def device_at(x, y, z, c):
    x, y, z = lax.rem(x, 4), lax.rem(y, 4), lax.rem(z, 8)
    return {"blk": z * 4 + lax.rem(x, 2) * 2 + c, "group": y * 2 + x // 2}


def remote(src, dst, send, recv, device):
    return pltpu.make_async_remote_copy(
        src_ref=src,
        dst_ref=dst,
        send_sem=send,
        recv_sem=recv,
        device_id=device,
        device_id_type=pl.DeviceIdType.MESH,
    )


def landed(ref, sem):
    pltpu.make_async_copy(ref, ref, sem).wait()


def kernel(
    scale,
    sharp_hbm,
    off_hbm,
    gain_i,
    gain_t,
    feat_i,
    feat_t,
    w_i,
    w_t,
    gi_out,
    gt_out,
    wi_out,
    wt_out,
    sharp_ref,
    off_ref,
    gain_v,
    small_sem,
    feats,
    weights,
    gains,
    act,
    act_t,
    unit,
    inv_norm,
    mean_s,
    rstd_s,
    imgs,
    txts,
    coef,
    d_own,
    d_txt,
    di_send,
    di_recv,
    di_pass,
    dt_send,
    dt_recv,
    dp,
    d_act,
    wb,
    w_pass,
    wr1,
    s1,
    wr2,
    s2,
    wr3,
    load_sem,
    i_send,
    i_recv,
    t_send,
    t_recv,
    a_sem,
    di_ss,
    di_rs,
    dt_ss,
    dt_rs,
    dp_ss,
    dp_rs,
    w1_ss,
    w1_rs,
    w2_ss,
    w2_rs,
    w3_ss,
    w3_rs,
    turn,
):
    k = lax.axis_index("blk")
    g = lax.axis_index("group")
    c = lax.rem(k, 2)
    z = k // 4
    xl = lax.rem(k // 2, 2)
    y = g // 2
    xh = lax.rem(g, 2)
    x = 2 * xh + xl
    oc = 1 - c
    ox = 1 - xh
    other = {"blk": k + 1 - 2 * c, "group": g}
    partner = {"blk": k, "group": y * 2 + ox}
    behind = lax.rem(k + 31, 32)
    ahead = lax.rem(k + 1, 32)
    linked = lax.rem(k + 31 + 2 * c, 32)
    rows, width = feats.shape[1], feats.shape[2]
    emb = imgs.shape[2]

    small = [
        pltpu.make_async_copy(src, dst, small_sem.at[n])
        for n, (src, dst) in enumerate(
            (
                (gain_t, gain_v.at[1]),
                (gain_i, gain_v.at[0]),
                (sharp_hbm, sharp_ref),
                (off_hbm, off_ref),
            )
        )
    ]
    for load in small:
        load.start()
    loads = [
        pltpu.make_async_copy(feat_t, feats.at[1], load_sem.at[0]),
        pltpu.make_async_copy(w_t, weights.at[1], load_sem.at[1]),
        pltpu.make_async_copy(feat_i, feats.at[0], load_sem.at[2]),
        pltpu.make_async_copy(w_i, weights.at[0], load_sem.at[3]),
    ]
    for n in (0, 2, 1, 3):
        loads[n].start()

    barrier = pltpu.get_barrier_semaphore()
    partners = [device_at(x, y + d, z, c) for d in (1, 2, 3)]
    partners += [device_at(x + d, y, z, c) for d in (1, 2, 3)]
    partners += [device_at(x, y, z + d, c) for d in range(1, 8)]
    partners += [device_at(x, y, z + d, oc) for d in range(8)]
    partners += [{"blk": linked, "group": y * 2 + j} for j in (0, 1)]
    for device in partners:
        pl.semaphore_signal(
            barrier, inc=1, device_id=device, device_id_type=pl.DeviceIdType.MESH
        )
    for load in small:
        load.wait()
    gains[0] = gain_v[0].reshape(1, width)
    gains[1] = gain_v[1].reshape(1, width)

    step = 32

    def normalize(t, wait_features):
        wait_features.wait()
        place = jnp.where(c == t, 0, 2)

        def body(i, _):
            r = pl.ds(pl.multiple_of(i * step, step), step)
            v = feats[t, r, :].astype(F32)
            mu = jnp.mean(v, axis=-1, keepdims=True)
            cen = v - mu
            rstd = lax.rsqrt(jnp.mean(cen * cen, axis=-1, keepdims=True) + 1e-06)
            mean_s[t, r, :] = mu
            rstd_s[t, r, :] = rstd
            act[place, r, :] = (cen * rstd * gains[t]).astype(BF)
            return 0

        lax.fori_loop(0, rows // step, body, 0, unroll=UNROLL)

    def project(t, wait_weights, dst):
        wait_weights.wait()
        place = jnp.where(c == t, 0, 2)
        for n in range(emb // 256):
            cols = slice(n * 256, (n + 1) * 256)
            unit[t, :, cols] = jnp.dot(
                act[place], weights[t, :, cols], preferred_element_type=F32
            )

        def body(i, _):
            r = pl.ds(pl.multiple_of(i * step, step), step)
            p = unit[t, r, :]
            inv = lax.rsqrt(jnp.sum(p * p, axis=-1, keepdims=True) + 1e-06)
            u = p * inv
            unit[t, r, :] = u
            inv_norm[t, r, :] = inv
            dst[r, :] = u.astype(BF)
            return 0

        lax.fori_loop(0, rows // step, body, 0, unroll=UNROLL)

    normalize(1, loads[0])
    normalize(0, loads[2])
    project(1, loads[1], txts.at[2 + xh])
    pl.semaphore_wait(barrier, 23)

    own_text = txts.at[2 + xh]
    other_text = txts.at[2 + ox]
    t_copies = [
        remote(
            own_text,
            txts.at[xh],
            t_send.at[0],
            t_recv.at[xh],
            {"blk": ahead, "group": g},
        ),
        remote(own_text, txts.at[2 + xh], t_send.at[1], t_recv.at[2], partner),
    ]
    t_copies[0].start()
    direct_text = remote(
        own_text,
        txts.at[xh],
        t_send.at[2],
        t_recv.at[xh],
        {"blk": ahead, "group": y * 2 + ox},
    )
    forward_text = remote(
        other_text,
        txts.at[ox],
        t_send.at[2],
        t_recv.at[ox],
        {"blk": ahead, "group": g},
    )

    @pl.when(c == 1)
    def _():
        direct_text.start()

    @pl.when(c == 0)
    def _():
        t_copies[1].start()

    project(0, loads[3], imgs.at[0])
    half_a, half_b = pl.ds(0, rows // 2), pl.ds(rows // 2, rows // 2)
    up, down = device_at(x, y + 1, z, c), device_at(x, y + 3, z, c)
    i_copies = [
        remote(
            imgs.at[src, part], imgs.at[dst, part], i_send.at[n], i_recv.at[n], device
        )
        for n, (src, dst, part, device) in enumerate(
            (
                (0, 1, half_a, up),
                (0, 1, half_b, up),
                (0, 3, half_b, down),
                (0, 3, half_a, down),
                (1, 2, half_a, up),
                (3, 2, half_b, down),
            )
        )
    ]
    for n in (0, 2, 1, 3):
        i_copies[n].start()
    a_copy = remote(act.at[2], act.at[1], a_sem.at[0], a_sem.at[1], other)
    a_copy.start()

    sharp = sharp_ref[0]
    off = off_ref[0]
    own, late = 2 + xh, 2 + ox

    def pairs(*todo, matching=False):
        for s, t in todo:
            sim = lax.dot_general(imgs[s], txts[t], NT, preferred_element_type=F32)
            prob = jax.nn.sigmoid(sharp * sim + off)
            if matching:
                row = lax.broadcasted_iota(jnp.int32, (rows, rows), 0)
                col = lax.broadcasted_iota(jnp.int32, (rows, rows), 1)
                prob = prob - (row == col).astype(F32)
            coef[s, t] = prob.astype(BF)

    def text_terms(t, shards):
        total = lax.dot_general(
            coef[shards[0], t], imgs[shards[0]], TN, preferred_element_type=F32
        )
        for s in shards[1:]:
            total += lax.dot_general(
                coef[s, t], imgs[s], TN, preferred_element_type=F32
            )
        return total

    def image_terms(s, dst):
        for n in range(emb // 256):
            cols = slice(n * 256, (n + 1) * 256)
            d = jnp.dot(coef[s, 0], txts[0, :, cols], preferred_element_type=F32)
            for t in range(1, 4):
                d += jnp.dot(coef[s, t], txts[t, :, cols], preferred_element_type=F32)
            dst[:, cols] = d.astype(dst.dtype)

    quarters = [pl.ds(n * rows // 4, rows // 4) for n in range(4)]
    di_copies = [
        remote(src, dst, di_ss.at[n], di_rs.at[n], device)
        for n, (src, dst, device) in enumerate(
            (
                (di_send.at[2, half_b], di_recv.at[0, half_b], up),
                (di_send.at[1, quarters[0]], di_pass.at[quarters[0]], up),
                (di_send.at[1, quarters[1]], di_pass.at[quarters[1]], up),
                (di_send.at[2, quarters[0]], di_recv.at[0, quarters[0]], up),
                (di_send.at[2, quarters[1]], di_recv.at[0, quarters[1]], up),
                (di_send.at[0, half_a], di_recv.at[1, half_a], down),
                (di_send.at[1, quarters[2]], di_pass.at[quarters[2]], down),
                (di_send.at[1, quarters[3]], di_pass.at[quarters[3]], down),
                (di_send.at[0, quarters[2]], di_recv.at[1, quarters[2]], down),
                (di_send.at[0, quarters[3]], di_recv.at[1, quarters[3]], down),
            )
        )
    ]
    def prev_copy(j):
        slot = jnp.where(c == 0, xh, j)
        owner = {"blk": behind, "group": y * 2 + jnp.where(c == 0, j, xh)}
        return remote(
            dt_send.at[j], dt_recv.at[slot], dt_ss.at[j], dt_rs.at[slot], owner
        )

    def start_prev(j):
        prev_copy(j).start()

    dt_copies = [prev_copy(0), prev_copy(1)]
    dt_copies.append(
        remote(dt_send.at[2], dt_recv.at[2], dt_ss.at[2], dt_rs.at[2], partner)
    )

    pairs((0, own), matching=True)
    a_copy.wait()
    for half in (0, 1):
        for n in range(width // 256):
            cols = slice(n * 256, (n + 1) * 256)
            act_t[cols, half * rows : (half + 1) * rows] = act[half, :, cols].T
    i_copies[0].wait_recv()
    i_copies[4].start()
    i_copies[2].wait_recv()
    i_copies[5].start()

    @pl.when(c == 1)
    def _():
        t_copies[1].start()

    @pl.when(c == 0)
    def _():
        landed(other_text, t_recv.at[2])
        forward_text.start()

    landed(txts.at[xh], t_recv.at[xh])
    pairs((0, xh))
    i_copies[1].wait_recv()
    i_copies[3].wait_recv()
    pairs((3, own), (1, own), (3, xh), (1, xh))
    d_txt[xh] = text_terms(xh, (0, 1, 3))
    landed(txts.at[ox], t_recv.at[ox])
    pairs((0, ox), (3, ox), (1, ox))
    d_txt[ox] = text_terms(ox, (0, 1, 3))

    @pl.when(c == 1)
    def _():
        landed(other_text, t_recv.at[2])

    pairs((3, late), (1, late))
    image_terms(3, di_send.at[2])
    di_copies[0].start()
    image_terms(1, di_send.at[0])
    di_copies[5].start()
    i_copies[4].wait_recv()
    i_copies[5].wait_recv()
    pairs((2, ox))
    dt_send[ox] = (d_txt[ox] + text_terms(ox, (2,))).astype(BF)
    start_prev(ox)
    pairs((2, xh))
    dt_send[xh] = (d_txt[xh] + text_terms(xh, (2,))).astype(BF)
    start_prev(xh)
    pairs((2, own), (2, late), (0, late))
    image_terms(2, di_send.at[1])
    for n in (1, 6, 2, 7):
        di_copies[n].start()
    d_txt[late] = text_terms(late, (0, 1, 2, 3))

    @pl.when(c == 0)
    def _():
        landed(dt_recv.at[ox], dt_rs.at[ox])
        dt_send[2] = (d_txt[2 + ox] + dt_recv[ox].astype(F32)).astype(BF)
        dt_copies[2].start()

    @pl.when(c == 1)
    def _():
        dt_send[2] = d_txt[2 + ox].astype(BF)
        dt_copies[2].start()

    def head_backward(t, total):
        place = jnp.where(c == t, 0, 2)

        def body(i, _):
            r = pl.ds(pl.multiple_of(i * step, step), step)
            d = sharp * total(r)
            u = unit[t, r, :]
            dot = jnp.sum(u * d, axis=-1, keepdims=True)
            at = pl.ds(pl.multiple_of(place * rows + i * step, step), step)
            dp[at, :] = ((d - u * dot) * inv_norm[t, r, :]).astype(BF)
            return 0

        lax.fori_loop(0, rows // step, body, 0, unroll=UNROLL)

    def img_total(r):
        total = d_own[r, :]
        for n in range(2):
            total += di_recv[n, r, :].astype(F32)
        return total

    d_txt[own] = text_terms(own, (0, 1, 2, 3))
    image_terms(0, d_own)
    for n, slot in ((0, 2), (2, 0), (1, 2), (3, 0)):
        arrived, onward = ((1, 3), (2, 4), (6, 8), (7, 9))[n]
        di_copies[arrived].wait_recv()
        di_send[slot, quarters[n], :] = (
            di_send[slot, quarters[n], :].astype(F32)
            + di_pass[quarters[n], :].astype(F32)
        ).astype(BF)
        di_copies[onward].start()
    for n in (0, 5, 3, 8, 4, 9):
        di_copies[n].wait_recv()
    head_backward(0, img_total)
    img_order = [lax.rem(y + d, 4) for d in (2, 1, 3, 0)]
    txt_order = (0, 2, 1, 3)

    def columns(j, core):
        n = jnp.where(core == 0, img_order[j], txt_order[j])
        return pl.ds(pl.multiple_of(n * 256, 256), 256)

    dp_copies = [
        remote(
            dp.at[pl.ds(2 * rows, rows), columns(j, oc)],
            dp.at[pl.ds(rows, rows), columns(j, oc)],
            dp_ss.at[j],
            dp_rs.at[j],
            other,
        )
        for j in range(4)
    ]

    @pl.when(c == 1)
    def _():
        for copy in dp_copies:
            copy.start()

    landed(dt_recv.at[2], dt_rs.at[2])
    landed(dt_recv.at[xh], dt_rs.at[xh])

    @pl.when(c == 1)
    def _():
        landed(dt_recv.at[ox], dt_rs.at[ox])

    first = jnp.where(c == 0, xh, 0)
    both = c.astype(F32)

    def txt_total(r):
        total = d_txt[2 + xh, r, :] + dt_recv[2, r, :].astype(F32)
        total += dt_recv[first, r, :].astype(F32)
        return total + both * dt_recv[1, r, :].astype(F32)

    head_backward(1, txt_total)

    @pl.when(c == 0)
    def _():
        for copy in dp_copies:
            copy.start()


    def along_a(d):
        return device_at(
            jnp.where(c == 0, x, x + d), jnp.where(c == 0, y + d, y), z, c
        )

    pos_a = jnp.where(c == 0, y, x)
    pos_b = jnp.where(c == 0, x, y)
    fore, aft, far = (lax.rem(pos_a + d, 4) for d in (1, 3, 2))

    pieces = (
        [(wb.at[far, b], w_pass.at[b], along_a(1)) for b in (0, 1)]
        + [(wb.at[fore, b], wr1.at[0, b], along_a(1)) for b in (2, 3, 0, 1)]
        + [(wb.at[far, b], w_pass.at[b], along_a(3)) for b in (2, 3)]
        + [(wb.at[aft, b], wr1.at[1, b], along_a(3)) for b in (0, 1, 2, 3)]
    )
    w1 = [
        remote(src, dst, w1_ss.at[n], w1_rs.at[n], device)
        for n, (src, dst, device) in enumerate(pieces)
    ]

    for j in range(4):
        n = jnp.where(c == 0, img_order[j], txt_order[j])
        cols = columns(j, c)
        landed(dp.at[pl.ds(rows, rows), cols], dp_rs.at[j])
        part = jnp.dot(
            act_t[...], dp[0 : 2 * rows, cols], preferred_element_type=F32
        )
        part = part.astype(BF).reshape(8, 2, 2, 48, 256)
        for xhi in range(2):
            for xlo in range(2):
                px = 2 * xhi + xlo
                wb[jnp.where(c == 0, n, px), jnp.where(c == 0, px, n)] = part[
                    :, xlo, :, :, xhi * 128 : (xhi + 1) * 128
                ]

        @pl.when(c == 0)
        def _():
            for n in ((0, 6, 1, 7), (2,), (8,), ())[j]:
                w1[n].start()

        @pl.when(c == 1)
        def _():
            for n in ((0, 8), (6, 2), (1,), (7,))[j]:
                w1[n].start()

    def features_backward(t, out):
        place = jnp.where(c == t, 0, 2)
        dproj = dp[pl.ds(pl.multiple_of(place * rows, rows), rows), :]
        for n in range(width // 256):
            cols = slice(n * 256, (n + 1) * 256)
            d_act[:, cols] = lax.dot_general(
                dproj, weights[t, cols, :], NT, preferred_element_type=F32
            )

        def body(i, _):
            r = pl.ds(pl.multiple_of(i * step, step), step)
            rstd = rstd_s[t, r, :]
            xhat = (feats[t, r, :].astype(F32) - mean_s[t, r, :]) * rstd
            ghat = d_act[r, :] * gains[t]
            m1 = jnp.mean(ghat, axis=-1, keepdims=True)
            m2 = jnp.mean(ghat * xhat, axis=-1, keepdims=True)
            out[r, :] = rstd * (ghat - m1 - xhat * m2)
            return 0

        lax.fori_loop(0, rows // step, body, 0, unroll=UNROLL)

    features_backward(0, gi_out)
    for b, arrived, onward, chunk in (
        (0, 0, 4, fore),
        (2, 6, 10, aft),
        (1, 1, 5, fore),
        (3, 7, 11, aft),
    ):
        w1[arrived].wait_recv()
        for zz in range(8):
            wb[chunk, b, zz] = (
                wb[chunk, b, zz].astype(F32) + w_pass[b, zz].astype(F32)
            ).astype(BF)
        w1[onward].start()
        if b == 2:
            w1[3].start()
            w1[9].start()
    features_backward(1, gt_out)

    def w2_copy(b, slot, half, device):
        part = pl.ds(half * 4, 4)
        return remote(
            s1.at[b, part],
            wr2.at[slot, part],
            w2_ss.at[slot, half],
            w2_rs.at[slot, half],
            device,
        )

    def w2_start(b, half):
        device = device_at(jnp.where(c == 0, b, x), jnp.where(c == 0, y, b), z, c)
        w2_copy(b, lax.rem(b + 3 - pos_b, 4), half, device).start()

    for b, early, late_piece in ((0, 8, 4), (2, 2, 10), (1, 9, 5), (3, 3, 11)):
        w1[early].wait_recv()
        w1[late_piece].wait_recv()
        for zz in range(8):
            total = wb[pos_a, b, zz].astype(F32) + wr1[0, b, zz].astype(F32)
            s1[b, zz] = (total + wr1[1, b, zz].astype(F32)).astype(BF)

        if b == 2:
            for copy in w1:
                copy.wait_send()
            pl.semaphore_signal(
                turn, inc=1, device_id=other, device_id_type=pl.DeviceIdType.MESH
            )

    pl.semaphore_wait(turn, 1)
    for half in (0, 1):
        for b in (0, 2, 1, 3):

            @pl.when(pos_b != b)
            def _():
                w2_start(b, half)

    def w3_copy(zd, cd):
        return remote(
            s2.at[zd, cd],
            wr3.at[c, z],
            w3_ss.at[zd, cd],
            w3_rs.at[c, z],
            {"blk": zd * 4 + xl * 2 + cd, "group": g},
        )

    for half in (0, 1):
        for d in range(3):
            w2_copy(0, d, half, other).wait_recv()
        for zd in range(half * 4, half * 4 + 4):
            total = s1[pos_b, zd].astype(F32)
            for d in range(3):
                total += wr2[d, zd].astype(F32)
            s2[zd] = total.astype(BF)
            for cd in (0, 1):

                @pl.when((zd != z) | (cd != c))
                def _():
                    w3_copy(zd, cd).start()

    wr3[c, z] = s2[z, c]
    for t, out in ((0, wi_out), (1, wt_out)):
        for zs in range(8):

            @pl.when((zs != z) | (t != c))
            def _():
                landed(wr3.at[t, zs], w3_rs.at[t, zs])

        total = wr3[t, 0].astype(F32)
        for zs in range(1, 8):
            total += wr3[t, zs].astype(F32)
        out[...] = total * scale

    for copy in t_copies + [direct_text] + i_copies + di_copies + dt_copies:
        copy.wait_send()
    for copy in dp_copies:
        copy.wait_send()
    for half in (0, 1):
        for d in range(3):
            w2_copy(0, d, half, other).wait_send()
    for zd in range(8):
        for cd in (0, 1):

            @pl.when((zd != z) | (cd != c))
            def _():
                w3_copy(zd, cd).wait_send()


def hand_out(*refs):
    copies = [
        pltpu.make_async_copy(refs[n], refs[4 + n], refs[8].at[n]) for n in range(4)
    ]
    for copy in copies:
        copy.start()
    for copy in copies:
        copy.wait()


def on_device(feat_i, feat_t, gain_i, gain_t, w_i, w_t, sharp, off):
    rows, width = feat_i.shape
    emb = w_i.shape[1]
    batch = rows * lax.axis_size("group") * lax.axis_size("blk")
    scale = math.sqrt(emb / batch)
    vmem = pl.BlockSpec(memory_space=pltpu.VMEM)
    hbm = pl.BlockSpec(memory_space=pl.ANY)
    dma = pltpu.SemaphoreType.DMA
    grads = pl.pallas_call(
        functools.partial(kernel, scale),
        name="siglip_grads",
        out_shape=(
            pltpu.VMEM((rows, width), F32),
            pltpu.VMEM((rows, width), F32),
            pltpu.VMEM((48, 128), F32),
            pltpu.VMEM((48, 128), F32),
        ),
        in_specs=[hbm] * 8,
        out_specs=(vmem, vmem, vmem, vmem),
        scratch_shapes=[
            pltpu.SMEM((1,), F32),
            pltpu.SMEM((1,), F32),
            pltpu.VMEM((2, width), F32),
            dma((4,)),
            pltpu.VMEM((2, rows, width), BF),
            pltpu.VMEM((2, width, emb), BF),
            pltpu.VMEM((2, 1, width), F32),
            pltpu.VMEM((3, rows, width), BF),
            pltpu.VMEM((width, 2 * rows), BF),
            pltpu.VMEM((2, rows, emb), F32),
            pltpu.VMEM((2, rows, 1), F32),
            pltpu.VMEM((2, rows, 1), F32),
            pltpu.VMEM((2, rows, 1), F32),
            pltpu.VMEM((4, rows, emb), BF),
            pltpu.VMEM((4, rows, emb), BF),
            pltpu.VMEM((4, 4, rows, rows), BF),
            pltpu.VMEM((rows, emb), F32),
            pltpu.VMEM((4, rows, emb), F32),
            pltpu.VMEM((3, rows, emb), BF),
            pltpu.VMEM((2, rows, emb), BF),
            pltpu.VMEM((rows, emb), BF),
            pltpu.VMEM((3, rows, emb), BF),
            pltpu.VMEM((3, rows, emb), BF),
            pltpu.VMEM((3 * rows, emb), BF),
            pltpu.VMEM((rows, width), F32),
            pltpu.VMEM((4, 4, 8, 2, 48, 128), BF),
            pltpu.VMEM((4, 8, 2, 48, 128), BF),
            pltpu.VMEM((2, 4, 8, 2, 48, 128), BF),
            pltpu.VMEM((4, 8, 2, 48, 128), BF),
            pltpu.VMEM((3, 8, 2, 48, 128), BF),
            pltpu.VMEM((8, 2, 48, 128), BF),
            pltpu.VMEM((2, 8, 48, 128), BF),
            dma((4,)),
            dma((6,)),
            dma((6,)),
            dma((3,)),
            dma((3,)),
            dma((2,)),
            dma((10,)),
            dma((10,)),
            dma((3,)),
            dma((3,)),
            dma((4,)),
            dma((4,)),
            dma((12,)),
            dma((12,)),
            dma((3, 2)),
            dma((3, 2)),
            dma((8, 2)),
            dma((2, 8)),
            pltpu.SemaphoreType.REGULAR,
        ],
        compiler_params=pltpu.CompilerParams(
            collective_id=0, has_side_effects=True, vmem_limit_bytes=54 << 20
        ),
        cost_estimate=pl.CostEstimate(
            flops=11 * 10**9, bytes_accessed=11 * 10**6, transcendentals=10**6
        ),
    )(
        sharp,
        off,
        gain_i,
        gain_t,
        feat_i,
        feat_t,
        w_i,
        w_t,
    )
    return pl.pallas_call(
        hand_out,
        name="hand_out",
        out_shape=tuple(jax.ShapeDtypeStruct(a.shape, a.dtype) for a in grads),
        in_specs=[hbm] * 4,
        out_specs=(hbm,) * 4,
        scratch_shapes=[dma((4,))],
        compiler_params=pltpu.CompilerParams(vmem_limit_bytes=1 << 20),
    )(*grads)


def solution(mesh):
    rows = P(("blk", "group"), None)
    return jax.shard_map(
        on_device,
        mesh=mesh,
        in_specs=(rows, rows, P(), P(), P(), P(), P(), P()),
        out_specs=(rows, rows, P("blk", "group"), P("blk", "group")),
        check_vma=False,
    )
```

```python
import functools
import math

import jax
import jax.numpy as jnp
from jax import lax
from jax.experimental import pallas as pl
from jax.experimental.pallas import tpu as pltpu
from jax.sharding import PartitionSpec as P

BF = jnp.bfloat16
UNROLL = 8
F32 = jnp.float32
NT = (((1,), (1,)), ((), ()))
TN = (((0,), (0,)), ((), ()))


def device_at(x, y, z, c):
    x, y, z = lax.rem(x, 4), lax.rem(y, 4), lax.rem(z, 8)
    return {"blk": z * 4 + lax.rem(x, 2) * 2 + c, "group": y * 2 + x // 2}


def remote(src, dst, send, recv, device):
    return pltpu.make_async_remote_copy(
        src_ref=src,
        dst_ref=dst,
        send_sem=send,
        recv_sem=recv,
        device_id=device,
        device_id_type=pl.DeviceIdType.MESH,
    )


def landed(ref, sem):
    pltpu.make_async_copy(ref, ref, sem).wait()


def kernel(
    scale,
    sharp_hbm,
    off_hbm,
    gain_i,
    gain_t,
    feat_i,
    feat_t,
    w_i,
    w_t,
    gi_out,
    gt_out,
    wi_out,
    wt_out,
    sharp_ref,
    off_ref,
    gain_v,
    small_sem,
    feats,
    weights,
    gains,
    act,
    act_t,
    unit,
    inv_norm,
    mean_s,
    rstd_s,
    imgs,
    txts,
    coef,
    d_own,
    d_txt,
    di_send,
    di_recv,
    di_pass,
    dt_send,
    dt_recv,
    dp,
    d_act,
    wb,
    w_pass,
    wr1,
    s1,
    wr2,
    s2,
    wr3,
    wz,
    rz,
    sa,
    ra,
    sb,
    rb,
    top,
    wz_ss,
    wz_rs,
    ra_ss,
    ra_rs,
    rb_ss,
    rb_rs,
    top_sem,
    load_sem,
    i_send,
    i_recv,
    t_send,
    t_recv,
    a_sem,
    di_ss,
    di_rs,
    dt_ss,
    dt_rs,
    dp_ss,
    dp_rs,
    w1_ss,
    w1_rs,
    w2_ss,
    w2_rs,
    w3_ss,
    w3_rs,
    turn,
):
    k = lax.axis_index("blk")
    g = lax.axis_index("group")
    c = lax.rem(k, 2)
    z = k // 4
    xl = lax.rem(k // 2, 2)
    y = g // 2
    xh = lax.rem(g, 2)
    x = 2 * xh + xl
    oc = 1 - c
    ox = 1 - xh
    other = {"blk": k + 1 - 2 * c, "group": g}
    partner = {"blk": k, "group": y * 2 + ox}
    behind = lax.rem(k + 31, 32)
    ahead = lax.rem(k + 1, 32)
    linked = lax.rem(k + 31 + 2 * c, 32)
    rows, width = feats.shape[1], feats.shape[2]
    emb = imgs.shape[2]

    small = [
        pltpu.make_async_copy(src, dst, small_sem.at[n])
        for n, (src, dst) in enumerate(
            (
                (gain_t, gain_v.at[1]),
                (gain_i, gain_v.at[0]),
                (sharp_hbm, sharp_ref),
                (off_hbm, off_ref),
            )
        )
    ]
    for load in small:
        load.start()
    loads = [
        pltpu.make_async_copy(feat_t, feats.at[1], load_sem.at[0]),
        pltpu.make_async_copy(w_t, weights.at[1], load_sem.at[1]),
        pltpu.make_async_copy(feat_i, feats.at[0], load_sem.at[2]),
        pltpu.make_async_copy(w_i, weights.at[0], load_sem.at[3]),
    ]
    for n in (0, 2, 1, 3):
        loads[n].start()

    barrier = pltpu.get_barrier_semaphore()
    partners = [device_at(x, y + d, z, c) for d in (1, 2, 3)]
    partners += [device_at(x + d, y, z, c) for d in (1, 2, 3)]
    partners += [device_at(x, y, z + d, c) for d in range(1, 8)]
    partners += [device_at(x, y, z + d, oc) for d in range(8)]
    partners += [{"blk": linked, "group": y * 2 + j} for j in (0, 1)]
    for device in partners:
        pl.semaphore_signal(
            barrier, inc=1, device_id=device, device_id_type=pl.DeviceIdType.MESH
        )
    for load in small:
        load.wait()
    gains[0] = gain_v[0].reshape(1, width)
    gains[1] = gain_v[1].reshape(1, width)

    step = 32

    def normalize(t, wait_features):
        wait_features.wait()
        place = jnp.where(c == t, 0, 2)

        def body(i, _):
            r = pl.ds(pl.multiple_of(i * step, step), step)
            v = feats[t, r, :].astype(F32)
            mu = jnp.mean(v, axis=-1, keepdims=True)
            cen = v - mu
            rstd = lax.rsqrt(jnp.mean(cen * cen, axis=-1, keepdims=True) + 1e-06)
            mean_s[t, r, :] = mu
            rstd_s[t, r, :] = rstd
            act[place, r, :] = (cen * rstd * gains[t]).astype(BF)
            return 0

        lax.fori_loop(0, rows // step, body, 0, unroll=UNROLL)

    def project(t, wait_weights, dst):
        wait_weights.wait()
        place = jnp.where(c == t, 0, 2)
        for n in range(emb // 256):
            cols = slice(n * 256, (n + 1) * 256)
            unit[t, :, cols] = jnp.dot(
                act[place], weights[t, :, cols], preferred_element_type=F32
            )

        def body(i, _):
            r = pl.ds(pl.multiple_of(i * step, step), step)
            p = unit[t, r, :]
            inv = lax.rsqrt(jnp.sum(p * p, axis=-1, keepdims=True) + 1e-06)
            u = p * inv
            unit[t, r, :] = u
            inv_norm[t, r, :] = inv
            dst[r, :] = u.astype(BF)
            return 0

        lax.fori_loop(0, rows // step, body, 0, unroll=UNROLL)

    normalize(1, loads[0])
    normalize(0, loads[2])
    project(1, loads[1], txts.at[2 + xh])
    pl.semaphore_wait(barrier, 23)

    own_text = txts.at[2 + xh]
    other_text = txts.at[2 + ox]
    t_copies = [
        remote(
            own_text,
            txts.at[xh],
            t_send.at[0],
            t_recv.at[xh],
            {"blk": ahead, "group": g},
        ),
        remote(own_text, txts.at[2 + xh], t_send.at[1], t_recv.at[2], partner),
    ]
    t_copies[0].start()
    direct_text = remote(
        own_text,
        txts.at[xh],
        t_send.at[2],
        t_recv.at[xh],
        {"blk": ahead, "group": y * 2 + ox},
    )
    forward_text = remote(
        other_text,
        txts.at[ox],
        t_send.at[2],
        t_recv.at[ox],
        {"blk": ahead, "group": g},
    )

    @pl.when(c == 1)
    def _():
        direct_text.start()

    @pl.when(c == 0)
    def _():
        t_copies[1].start()

    project(0, loads[3], imgs.at[0])
    half_a, half_b = pl.ds(0, rows // 2), pl.ds(rows // 2, rows // 2)
    up, down = device_at(x, y + 1, z, c), device_at(x, y + 3, z, c)
    i_copies = [
        remote(
            imgs.at[src, part], imgs.at[dst, part], i_send.at[n], i_recv.at[n], device
        )
        for n, (src, dst, part, device) in enumerate(
            (
                (0, 1, half_a, up),
                (0, 1, half_b, up),
                (0, 3, half_b, down),
                (0, 3, half_a, down),
                (1, 2, half_a, up),
                (3, 2, half_b, down),
            )
        )
    ]
    for n in (0, 2, 1, 3):
        i_copies[n].start()
    a_copy = remote(act.at[2], act.at[1], a_sem.at[0], a_sem.at[1], other)
    a_copy.start()

    sharp = sharp_ref[0]
    off = off_ref[0]
    own, late = 2 + xh, 2 + ox

    def pairs(*todo, matching=False):
        for s, t in todo:
            sim = lax.dot_general(imgs[s], txts[t], NT, preferred_element_type=F32)
            prob = jax.nn.sigmoid(sharp * sim + off)
            if matching:
                row = lax.broadcasted_iota(jnp.int32, (rows, rows), 0)
                col = lax.broadcasted_iota(jnp.int32, (rows, rows), 1)
                prob = prob - (row == col).astype(F32)
            coef[s, t] = prob.astype(BF)

    def text_terms(t, shards):
        total = lax.dot_general(
            coef[shards[0], t], imgs[shards[0]], TN, preferred_element_type=F32
        )
        for s in shards[1:]:
            total += lax.dot_general(
                coef[s, t], imgs[s], TN, preferred_element_type=F32
            )
        return total

    def image_terms(s, dst):
        for n in range(emb // 256):
            cols = slice(n * 256, (n + 1) * 256)
            d = jnp.dot(coef[s, 0], txts[0, :, cols], preferred_element_type=F32)
            for t in range(1, 4):
                d += jnp.dot(coef[s, t], txts[t, :, cols], preferred_element_type=F32)
            dst[:, cols] = d.astype(dst.dtype)

    quarters = [pl.ds(n * rows // 4, rows // 4) for n in range(4)]
    di_copies = [
        remote(src, dst, di_ss.at[n], di_rs.at[n], device)
        for n, (src, dst, device) in enumerate(
            (
                (di_send.at[2, half_b], di_recv.at[0, half_b], up),
                (di_send.at[1, quarters[0]], di_pass.at[quarters[0]], up),
                (di_send.at[1, quarters[1]], di_pass.at[quarters[1]], up),
                (di_send.at[2, quarters[0]], di_recv.at[0, quarters[0]], up),
                (di_send.at[2, quarters[1]], di_recv.at[0, quarters[1]], up),
                (di_send.at[0, half_a], di_recv.at[1, half_a], down),
                (di_send.at[1, quarters[2]], di_pass.at[quarters[2]], down),
                (di_send.at[1, quarters[3]], di_pass.at[quarters[3]], down),
                (di_send.at[0, quarters[2]], di_recv.at[1, quarters[2]], down),
                (di_send.at[0, quarters[3]], di_recv.at[1, quarters[3]], down),
            )
        )
    ]
    def prev_copy(j):
        slot = jnp.where(c == 0, xh, j)
        owner = {"blk": behind, "group": y * 2 + jnp.where(c == 0, j, xh)}
        return remote(
            dt_send.at[j], dt_recv.at[slot], dt_ss.at[j], dt_rs.at[slot], owner
        )

    def start_prev(j):
        prev_copy(j).start()

    dt_copies = [prev_copy(0), prev_copy(1)]
    dt_copies.append(
        remote(dt_send.at[2], dt_recv.at[2], dt_ss.at[2], dt_rs.at[2], partner)
    )

    pairs((0, own), matching=True)
    a_copy.wait()
    for half in (0, 1):
        for n in range(width // 256):
            cols = slice(n * 256, (n + 1) * 256)
            act_t[cols, half * rows : (half + 1) * rows] = act[half, :, cols].T
    i_copies[0].wait_recv()
    i_copies[4].start()
    i_copies[2].wait_recv()
    i_copies[5].start()

    @pl.when(c == 1)
    def _():
        t_copies[1].start()

    @pl.when(c == 0)
    def _():
        landed(other_text, t_recv.at[2])
        forward_text.start()

    landed(txts.at[xh], t_recv.at[xh])
    pairs((0, xh))
    i_copies[1].wait_recv()
    i_copies[3].wait_recv()
    pairs((3, own), (1, own), (3, xh), (1, xh))
    d_txt[xh] = text_terms(xh, (0, 1, 3))
    landed(txts.at[ox], t_recv.at[ox])
    pairs((0, ox), (3, ox), (1, ox))
    d_txt[ox] = text_terms(ox, (0, 1, 3))

    @pl.when(c == 1)
    def _():
        landed(other_text, t_recv.at[2])

    pairs((3, late), (1, late))
    image_terms(3, di_send.at[2])
    di_copies[0].start()
    image_terms(1, di_send.at[0])
    di_copies[5].start()
    i_copies[4].wait_recv()
    i_copies[5].wait_recv()
    pairs((2, ox))
    dt_send[ox] = (d_txt[ox] + text_terms(ox, (2,))).astype(BF)
    start_prev(ox)
    pairs((2, xh))
    dt_send[xh] = (d_txt[xh] + text_terms(xh, (2,))).astype(BF)
    start_prev(xh)
    pairs((2, own), (2, late), (0, late))
    image_terms(2, di_send.at[1])
    for n in (1, 6, 2, 7):
        di_copies[n].start()
    d_txt[late] = text_terms(late, (0, 1, 2, 3))

    @pl.when(c == 0)
    def _():
        landed(dt_recv.at[ox], dt_rs.at[ox])
        dt_send[2] = (d_txt[2 + ox] + dt_recv[ox].astype(F32)).astype(BF)
        dt_copies[2].start()

    @pl.when(c == 1)
    def _():
        dt_send[2] = d_txt[2 + ox].astype(BF)
        dt_copies[2].start()

    def head_backward(t, total):
        place = jnp.where(c == t, 0, 2)

        def body(i, _):
            r = pl.ds(pl.multiple_of(i * step, step), step)
            d = sharp * total(r)
            u = unit[t, r, :]
            dot = jnp.sum(u * d, axis=-1, keepdims=True)
            at = pl.ds(pl.multiple_of(place * rows + i * step, step), step)
            dp[at, :] = ((d - u * dot) * inv_norm[t, r, :]).astype(BF)
            return 0

        lax.fori_loop(0, rows // step, body, 0, unroll=UNROLL)

    def img_total(r):
        total = d_own[r, :]
        for n in range(2):
            total += di_recv[n, r, :].astype(F32)
        return total

    d_txt[own] = text_terms(own, (0, 1, 2, 3))
    image_terms(0, d_own)
    for n, slot in ((0, 2), (2, 0), (1, 2), (3, 0)):
        arrived, onward = ((1, 3), (2, 4), (6, 8), (7, 9))[n]
        di_copies[arrived].wait_recv()
        di_send[slot, quarters[n], :] = (
            di_send[slot, quarters[n], :].astype(F32)
            + di_pass[quarters[n], :].astype(F32)
        ).astype(BF)
        di_copies[onward].start()
    for n in (0, 5, 3, 8, 4, 9):
        di_copies[n].wait_recv()
    head_backward(0, img_total)
    img_order = [lax.rem(y + d, 4) for d in (2, 1, 3, 0)]
    txt_order = (0, 2, 1, 3)

    def columns(j, core):
        n = jnp.where(core == 0, img_order[j], txt_order[j])
        return pl.ds(pl.multiple_of(n * 256, 256), 256)

    dp_copies = [
        remote(
            dp.at[pl.ds(2 * rows, rows), columns(j, oc)],
            dp.at[pl.ds(rows, rows), columns(j, oc)],
            dp_ss.at[j],
            dp_rs.at[j],
            other,
        )
        for j in range(4)
    ]

    @pl.when(c == 1)
    def _():
        for copy in dp_copies:
            copy.start()

    landed(dt_recv.at[2], dt_rs.at[2])
    landed(dt_recv.at[xh], dt_rs.at[xh])

    @pl.when(c == 1)
    def _():
        landed(dt_recv.at[ox], dt_rs.at[ox])

    first = jnp.where(c == 0, xh, 0)
    both = c.astype(F32)

    def txt_total(r):
        total = d_txt[2 + xh, r, :] + dt_recv[2, r, :].astype(F32)
        total += dt_recv[first, r, :].astype(F32)
        return total + both * dt_recv[1, r, :].astype(F32)

    head_backward(1, txt_total)

    @pl.when(c == 0)
    def _():
        for copy in dp_copies:
            copy.start()


    def along_a(d):
        return device_at(
            jnp.where(c == 0, x, x + d), jnp.where(c == 0, y + d, y), z, c
        )

    pos_a = jnp.where(c == 0, y, x)
    pos_b = jnp.where(c == 0, x, y)
    fore, aft, far = (lax.rem(pos_a + d, 4) for d in (1, 3, 2))

    pieces = (
        [(wb.at[far, b], w_pass.at[b], along_a(1)) for b in (0, 1)]
        + [(wb.at[fore, b], wr1.at[0, b], along_a(1)) for b in (2, 3, 0, 1)]
        + [(wb.at[far, b], w_pass.at[b], along_a(3)) for b in (2, 3)]
        + [(wb.at[aft, b], wr1.at[1, b], along_a(3)) for b in (0, 1, 2, 3)]
    )
    w1 = [
        remote(src, dst, w1_ss.at[n], w1_rs.at[n], device)
        for n, (src, dst, device) in enumerate(pieces)
    ]

    for j in range(4):
        n = jnp.where(c == 0, img_order[j], txt_order[j])
        cols = columns(j, c)
        landed(dp.at[pl.ds(rows, rows), cols], dp_rs.at[j])
        part = jnp.dot(
            act_t[...], dp[0 : 2 * rows, cols], preferred_element_type=F32
        )
        part = part.astype(BF).reshape(8, 2, 96, 256)
        for xhi in range(2):
            for xlo in range(2):
                px = 2 * xhi + xlo
                at_a, at_b = jnp.where(c == 0, n, px), jnp.where(c == 0, px, n)
                block = part[:, xlo, :, xhi * 128 : (xhi + 1) * 128]
                wb[at_a, at_b] = block[:, 16:]
                wz[:, at_a, at_b] = block[:, :16]

        @pl.when(c == 0)
        def _():
            for n in ((0, 6, 1, 7), (2,), (8,), ())[j]:
                w1[n].start()

        @pl.when(c == 1)
        def _():
            for n in ((0, 8), (6, 2), (1,), (7,))[j]:
                w1[n].start()

    def features_backward(t, out):
        place = jnp.where(c == t, 0, 2)
        dproj = dp[pl.ds(pl.multiple_of(place * rows, rows), rows), :]
        for n in range(width // 256):
            cols = slice(n * 256, (n + 1) * 256)
            d_act[:, cols] = lax.dot_general(
                dproj, weights[t, cols, :], NT, preferred_element_type=F32
            )

        def body(i, _):
            r = pl.ds(pl.multiple_of(i * step, step), step)
            rstd = rstd_s[t, r, :]
            xhat = (feats[t, r, :].astype(F32) - mean_s[t, r, :]) * rstd
            ghat = d_act[r, :] * gains[t]
            m1 = jnp.mean(ghat, axis=-1, keepdims=True)
            m2 = jnp.mean(ghat * xhat, axis=-1, keepdims=True)
            out[r, :] = rstd * (ghat - m1 - xhat * m2)
            return 0

        lax.fori_loop(0, rows // step, body, 0, unroll=UNROLL)

    wz_copies = []
    for d in (4, 3, 5, 2, 6, 1, 7):
        wz_copies.append(
            remote(
                wz.at[lax.rem(z + d, 8)],
                rz.at[z],
                wz_ss.at[d - 1],
                wz_rs.at[z],
                device_at(x, y, z + d, c),
            )
        )
        wz_copies[-1].start()
    rz[z] = wz[z]
    features_backward(0, gi_out)
    for b, arrived, onward, chunk in (
        (0, 0, 4, fore),
        (2, 6, 10, aft),
        (1, 1, 5, fore),
        (3, 7, 11, aft),
    ):
        w1[arrived].wait_recv()
        for zz in range(8):
            wb[chunk, b, zz] = (
                wb[chunk, b, zz].astype(F32) + w_pass[b, zz].astype(F32)
            ).astype(BF)
        w1[onward].start()
        if b == 2:
            w1[3].start()
            w1[9].start()
    features_backward(1, gt_out)

    def w2_copy(b, slot, half, device):
        part = pl.ds(half * 4, 4)
        return remote(
            s1.at[b, part],
            wr2.at[slot, part],
            w2_ss.at[slot, half],
            w2_rs.at[slot, half],
            device,
        )

    def w2_start(b, half):
        device = device_at(jnp.where(c == 0, b, x), jnp.where(c == 0, y, b), z, c)
        w2_copy(b, lax.rem(b + 3 - pos_b, 4), half, device).start()

    for b, early, late_piece in ((0, 8, 4), (2, 2, 10), (1, 9, 5), (3, 3, 11)):
        w1[early].wait_recv()
        w1[late_piece].wait_recv()
        for zz in range(8):
            total = wb[pos_a, b, zz].astype(F32) + wr1[0, b, zz].astype(F32)
            s1[b, zz] = (total + wr1[1, b, zz].astype(F32)).astype(BF)

        if b == 2:
            for copy in w1:
                copy.wait_send()
            pl.semaphore_signal(
                turn, inc=1, device_id=other, device_id_type=pl.DeviceIdType.MESH
            )

    pl.semaphore_wait(turn, 1)
    for half in (0, 1):
        for b in (0, 2, 1, 3):

            @pl.when(pos_b != b)
            def _():
                w2_start(b, half)

    for d in range(1, 8):
        src = lax.rem(z + d, 8)
        landed(rz.at[src], wz_rs.at[src])
    for a in range(4):
        for b in range(4):
            total = rz[0, a, b].astype(F32)
            for zs in range(1, 8):
                total += rz[zs, a, b].astype(F32)
            sa[a, b] = total.astype(BF)
    small_copies = [
        remote(
            sa.at[lax.rem(pos_a + d, 4)],
            ra.at[d - 1],
            ra_ss.at[d - 1],
            ra_rs.at[d - 1],
            along_a(d),
        )
        for d in (2, 1, 3)
    ]
    for copy in small_copies:
        copy.start()

    def w3_copy(zd, cd):
        if cd == 0:
            src, dst = s2.at[zd, pl.ds(0, 32)], wr3.at[c, z, pl.ds(16, 32)]
        else:
            src, dst = s2.at[zd, pl.ds(32, 48)], wr3.at[c, z]
        return remote(
            src,
            dst,
            w3_ss.at[zd, cd],
            w3_rs.at[c, z],
            {"blk": zd * 4 + xl * 2 + cd, "group": g},
        )

    for half in (0, 1):
        for d in range(3):
            w2_copy(0, d, half, other).wait_recv()
        for zd in range(half * 4, half * 4 + 4):
            total = s1[pos_b, zd].astype(F32)
            for d in range(3):
                total += wr2[d, zd].astype(F32)
            s2[zd] = total.astype(BF)
            for cd in (0, 1):

                @pl.when((zd != z) | (cd != c))
                def _():
                    w3_copy(zd, cd).start()

    @pl.when(c == 0)
    def _():
        wr3[0, z, 16:48] = s2[z, 0:32]

    @pl.when(c == 1)
    def _():
        wr3[1, z] = s2[z, 32:80]

    for d in (1, 2, 3):
        landed(ra.at[d - 1], ra_rs.at[d - 1])
    for b in range(4):
        total = sa[pos_a, b].astype(F32)
        for d in range(3):
            total += ra[d, b].astype(F32)
        sb[b] = total.astype(BF)
    for d in (2, 1, 3):
        small_copies.append(
            remote(
                sb.at[lax.rem(pos_b + d, 4)],
                rb.at[d - 1],
                rb_ss.at[d - 1],
                rb_rs.at[d - 1],
                device_at(
                    jnp.where(c == 0, x + d, x), jnp.where(c == 0, y, y + d), z, c
                ),
            )
        )
        small_copies[-1].start()
    for d in (1, 2, 3):
        landed(rb.at[d - 1], rb_rs.at[d - 1])
    total = sb[pos_b].astype(F32)
    for d in range(3):
        total += rb[d].astype(F32)
    top[c] = total
    top_copy = remote(top.at[1], top.at[1], top_sem.at[0], top_sem.at[1], other)

    @pl.when(c == 1)
    def _():
        top_copy.start()
        for t, out in ((0, wi_out), (1, wt_out)):
            for zs in range(8):

                @pl.when((zs != z) | (t == 0))
                def _():
                    landed(wr3.at[t, zs], w3_rs.at[t, zs])

            total = wr3[t, 0].astype(F32)
            for zs in range(1, 8):
                total += wr3[t, zs].astype(F32)
            out[...] = total * scale
        top_copy.wait_send()

    @pl.when(c == 0)
    def _():
        top_copy.wait_recv()
        for t, out in ((0, wi_out), (1, wt_out)):
            for zs in range(8):

                @pl.when((zs != z) | (t == 1))
                def _():
                    landed(wr3.at[t, zs, pl.ds(16, 32)], w3_rs.at[t, zs])

            total = wr3[t, 0, 16:48].astype(F32)
            for zs in range(1, 8):
                total += wr3[t, zs, 16:48].astype(F32)
            out[16:48] = total * scale
            out[0:16] = top[t] * scale

    for copy in t_copies + [direct_text] + i_copies + di_copies + dt_copies:
        copy.wait_send()
    for copy in dp_copies + wz_copies + small_copies:
        copy.wait_send()
    for half in (0, 1):
        for d in range(3):
            w2_copy(0, d, half, other).wait_send()
    for zd in range(8):
        for cd in (0, 1):

            @pl.when((zd != z) | (cd != c))
            def _():
                w3_copy(zd, cd).wait_send()


def hand_out(*refs):
    copies = [
        pltpu.make_async_copy(refs[n], refs[4 + n], refs[8].at[n]) for n in range(4)
    ]
    for copy in copies:
        copy.start()
    for copy in copies:
        copy.wait()


def on_device(feat_i, feat_t, gain_i, gain_t, w_i, w_t, sharp, off):
    rows, width = feat_i.shape
    emb = w_i.shape[1]
    batch = rows * lax.axis_size("group") * lax.axis_size("blk")
    scale = math.sqrt(emb / batch)
    vmem = pl.BlockSpec(memory_space=pltpu.VMEM)
    hbm = pl.BlockSpec(memory_space=pl.ANY)
    dma = pltpu.SemaphoreType.DMA
    grads = pl.pallas_call(
        functools.partial(kernel, scale),
        name="siglip_grads",
        out_shape=(
            pltpu.VMEM((rows, width), F32),
            pltpu.VMEM((rows, width), F32),
            pltpu.VMEM((48, 128), F32),
            pltpu.VMEM((48, 128), F32),
        ),
        in_specs=[hbm] * 8,
        out_specs=(vmem, vmem, vmem, vmem),
        scratch_shapes=[
            pltpu.SMEM((1,), F32),
            pltpu.SMEM((1,), F32),
            pltpu.VMEM((2, width), F32),
            dma((4,)),
            pltpu.VMEM((2, rows, width), BF),
            pltpu.VMEM((2, width, emb), BF),
            pltpu.VMEM((2, 1, width), F32),
            pltpu.VMEM((3, rows, width), BF),
            pltpu.VMEM((width, 2 * rows), BF),
            pltpu.VMEM((2, rows, emb), F32),
            pltpu.VMEM((2, rows, 1), F32),
            pltpu.VMEM((2, rows, 1), F32),
            pltpu.VMEM((2, rows, 1), F32),
            pltpu.VMEM((4, rows, emb), BF),
            pltpu.VMEM((4, rows, emb), BF),
            pltpu.VMEM((4, 4, rows, rows), BF),
            pltpu.VMEM((rows, emb), F32),
            pltpu.VMEM((4, rows, emb), F32),
            pltpu.VMEM((3, rows, emb), BF),
            pltpu.VMEM((2, rows, emb), BF),
            pltpu.VMEM((rows, emb), BF),
            pltpu.VMEM((3, rows, emb), BF),
            pltpu.VMEM((3, rows, emb), BF),
            pltpu.VMEM((3 * rows, emb), BF),
            pltpu.VMEM((rows, width), F32),
            pltpu.VMEM((4, 4, 8, 80, 128), BF),
            pltpu.VMEM((4, 8, 80, 128), BF),
            pltpu.VMEM((2, 4, 8, 80, 128), BF),
            pltpu.VMEM((4, 8, 80, 128), BF),
            pltpu.VMEM((3, 8, 80, 128), BF),
            pltpu.VMEM((8, 80, 128), BF),
            pltpu.VMEM((2, 8, 48, 128), BF),
            pltpu.VMEM((8, 4, 4, 16, 128), BF),
            pltpu.VMEM((8, 4, 4, 16, 128), BF),
            pltpu.VMEM((4, 4, 16, 128), BF),
            pltpu.VMEM((3, 4, 16, 128), BF),
            pltpu.VMEM((4, 16, 128), BF),
            pltpu.VMEM((3, 16, 128), BF),
            pltpu.VMEM((2, 16, 128), F32),
            dma((7,)),
            dma((8,)),
            dma((3,)),
            dma((3,)),
            dma((3,)),
            dma((3,)),
            dma((2,)),
            dma((4,)),
            dma((6,)),
            dma((6,)),
            dma((3,)),
            dma((3,)),
            dma((2,)),
            dma((10,)),
            dma((10,)),
            dma((3,)),
            dma((3,)),
            dma((4,)),
            dma((4,)),
            dma((12,)),
            dma((12,)),
            dma((3, 2)),
            dma((3, 2)),
            dma((8, 2)),
            dma((2, 8)),
            pltpu.SemaphoreType.REGULAR,
        ],
        compiler_params=pltpu.CompilerParams(
            collective_id=0, has_side_effects=True, vmem_limit_bytes=54 << 20
        ),
        cost_estimate=pl.CostEstimate(
            flops=11 * 10**9, bytes_accessed=11 * 10**6, transcendentals=10**6
        ),
    )(
        sharp,
        off,
        gain_i,
        gain_t,
        feat_i,
        feat_t,
        w_i,
        w_t,
    )
    return pl.pallas_call(
        hand_out,
        name="hand_out",
        out_shape=tuple(jax.ShapeDtypeStruct(a.shape, a.dtype) for a in grads),
        in_specs=[hbm] * 4,
        out_specs=(hbm,) * 4,
        scratch_shapes=[dma((4,))],
        compiler_params=pltpu.CompilerParams(vmem_limit_bytes=1 << 20),
    )(*grads)


def solution(mesh):
    rows = P(("blk", "group"), None)
    return jax.shard_map(
        on_device,
        mesh=mesh,
        in_specs=(rows, rows, P(), P(), P(), P(), P(), P()),
        out_specs=(rows, rows, P("blk", "group"), P("blk", "group")),
        check_vma=False,
    )
```

```python
import functools
import math

import jax
import jax.numpy as jnp
from jax import lax
from jax.experimental import pallas as pl
from jax.experimental.pallas import tpu as pltpu
from jax.sharding import PartitionSpec as P

BF = jnp.bfloat16
UNROLL = 8
F32 = jnp.float32
NT = (((1,), (1,)), ((), ()))
TN = (((0,), (0,)), ((), ()))


def device_at(x, y, z, c):
    x, y, z = lax.rem(x, 4), lax.rem(y, 4), lax.rem(z, 8)
    return {"blk": z * 4 + lax.rem(x, 2) * 2 + c, "group": y * 2 + x // 2}


def remote(src, dst, send, recv, device):
    return pltpu.make_async_remote_copy(
        src_ref=src,
        dst_ref=dst,
        send_sem=send,
        recv_sem=recv,
        device_id=device,
        device_id_type=pl.DeviceIdType.MESH,
    )


def landed(ref, sem):
    pltpu.make_async_copy(ref, ref, sem).wait()


def kernel(
    scale,
    sharp_hbm,
    off_hbm,
    gain_i,
    gain_t,
    feat_i,
    feat_t,
    w_i,
    w_t,
    gi_out,
    gt_out,
    wi_out,
    wt_out,
    sharp_ref,
    off_ref,
    gain_v,
    small_sem,
    feats,
    weights,
    gains,
    act,
    act_t,
    unit,
    inv_norm,
    mean_s,
    rstd_s,
    imgs,
    txts,
    coef,
    d_own,
    d_txt,
    di_send,
    di_recv,
    di_pass,
    dt_send,
    dt_recv,
    dp,
    d_act,
    wb,
    w_pass,
    wr1,
    s1,
    wr2,
    s2,
    wr3,
    wz,
    rz,
    sa,
    ra,
    sb,
    rb,
    top,
    wz_ss,
    wz_rs,
    ra_ss,
    ra_rs,
    rb_ss,
    rb_rs,
    top_sem,
    load_sem,
    i_send,
    i_recv,
    t_send,
    t_recv,
    a_sem,
    di_ss,
    di_rs,
    dt_ss,
    dt_rs,
    dp_ss,
    dp_rs,
    w1_ss,
    w1_rs,
    w2_ss,
    w2_rs,
    w3_ss,
    w3_rs,
    turn,
):
    k = lax.axis_index("blk")
    g = lax.axis_index("group")
    c = lax.rem(k, 2)
    z = k // 4
    xl = lax.rem(k // 2, 2)
    y = g // 2
    xh = lax.rem(g, 2)
    x = 2 * xh + xl
    oc = 1 - c
    ox = 1 - xh
    other = {"blk": k + 1 - 2 * c, "group": g}
    partner = {"blk": k, "group": y * 2 + ox}
    behind = lax.rem(k + 31, 32)
    ahead = lax.rem(k + 1, 32)
    linked = lax.rem(k + 31 + 2 * c, 32)
    rows, width = feats.shape[1], feats.shape[2]
    emb = imgs.shape[2]

    small = [
        pltpu.make_async_copy(src, dst, small_sem.at[n])
        for n, (src, dst) in enumerate(
            (
                (gain_t, gain_v.at[1]),
                (gain_i, gain_v.at[0]),
                (sharp_hbm, sharp_ref),
                (off_hbm, off_ref),
            )
        )
    ]
    for load in small:
        load.start()
    loads = [
        pltpu.make_async_copy(feat_t, feats.at[1], load_sem.at[0]),
        pltpu.make_async_copy(w_t, weights.at[1], load_sem.at[1]),
        pltpu.make_async_copy(feat_i, feats.at[0], load_sem.at[2]),
        pltpu.make_async_copy(w_i, weights.at[0], load_sem.at[3]),
    ]
    for n in (0, 2, 1):
        loads[n].start()

    barrier = pltpu.get_barrier_semaphore()
    partners = [device_at(x, y + d, z, c) for d in (1, 2, 3)]
    partners += [device_at(x + d, y, z, c) for d in (1, 2, 3)]
    partners += [device_at(x, y, z + d, c) for d in range(1, 8)]
    partners += [device_at(x, y, z + d, oc) for d in range(8)]
    partners += [{"blk": linked, "group": y * 2 + j} for j in (0, 1)]
    for device in partners:
        pl.semaphore_signal(
            barrier, inc=1, device_id=device, device_id_type=pl.DeviceIdType.MESH
        )
    for load in small:
        load.wait()
    gains[0] = gain_v[0].reshape(1, width)
    gains[1] = gain_v[1].reshape(1, width)

    step = 32

    def normalize(t, wait_features):
        wait_features.wait()
        place = jnp.where(c == t, 0, 2)

        def body(i, _):
            r = pl.ds(pl.multiple_of(i * step, step), step)
            v = feats[t, r, :].astype(F32)
            mu = jnp.mean(v, axis=-1, keepdims=True)
            cen = v - mu
            rstd = lax.rsqrt(jnp.mean(cen * cen, axis=-1, keepdims=True) + 1e-06)
            mean_s[t, r, :] = mu
            rstd_s[t, r, :] = rstd
            act[place, r, :] = (cen * rstd * gains[t]).astype(BF)
            return 0

        lax.fori_loop(0, rows // step, body, 0, unroll=UNROLL)

    def project(t, wait_weights, dst):
        wait_weights.wait()
        if t == 1:
            loads[3].start()
        place = jnp.where(c == t, 0, 2)
        for n in range(emb // 256):
            cols = slice(n * 256, (n + 1) * 256)
            unit[t, :, cols] = jnp.dot(
                act[place], weights[t, :, cols], preferred_element_type=F32
            )

        def body(i, _):
            r = pl.ds(pl.multiple_of(i * step, step), step)
            p = unit[t, r, :]
            inv = lax.rsqrt(jnp.sum(p * p, axis=-1, keepdims=True) + 1e-06)
            u = p * inv
            unit[t, r, :] = u
            inv_norm[t, r, :] = inv
            dst[r, :] = u.astype(BF)
            return 0

        lax.fori_loop(0, rows // step, body, 0, unroll=UNROLL)

    normalize(1, loads[0])
    normalize(0, loads[2])
    project(1, loads[1], txts.at[0])
    pl.semaphore_wait(barrier, 23)

    own_text = txts.at[0]
    other_text = txts.at[1]
    t_copies = [
        remote(
            own_text,
            txts.at[2],
            t_send.at[0],
            t_recv.at[0],
            {"blk": ahead, "group": g},
        ),
        remote(own_text, other_text, t_send.at[1], t_recv.at[2], partner),
    ]
    direct_text = remote(
        own_text,
        txts.at[3],
        t_send.at[2],
        t_recv.at[1],
        {"blk": ahead, "group": y * 2 + ox},
    )
    forward_text = remote(
        other_text,
        txts.at[3],
        t_send.at[2],
        t_recv.at[1],
        {"blk": ahead, "group": g},
    )

    @pl.when(c == 1)
    def _():
        direct_text.start()

    t_copies[0].start()

    @pl.when(c == 0)
    def _():
        t_copies[1].start()

    project(0, loads[3], imgs.at[0])
    half_a, half_b = pl.ds(0, rows // 2), pl.ds(rows // 2, rows // 2)
    up, down = device_at(x, y + 1, z, c), device_at(x, y + 3, z, c)
    i_copies = [
        remote(
            imgs.at[src, part], imgs.at[dst, part], i_send.at[n], i_recv.at[n], device
        )
        for n, (src, dst, part, device) in enumerate(
            (
                (0, 1, half_a, up),
                (0, 1, half_b, up),
                (0, 3, half_b, down),
                (0, 3, half_a, down),
                (1, 2, half_a, up),
                (3, 2, half_b, down),
            )
        )
    ]
    for n in (0, 2, 1, 3):
        i_copies[n].start()
    a_copy = remote(act.at[2], act.at[1], a_sem.at[0], a_sem.at[1], other)
    a_copy.start()

    sharp = sharp_ref[0]
    off = off_ref[0]
    own, late, prev, cross = 0, 1, 2, 3

    def pairs(*todo, matching=False):
        for s, t in todo:
            sim = lax.dot_general(imgs[s], txts[t], NT, preferred_element_type=F32)
            prob = jax.nn.sigmoid(sharp * sim + off)
            if matching:
                row = lax.broadcasted_iota(jnp.int32, (rows, rows), 0)
                col = lax.broadcasted_iota(jnp.int32, (rows, rows), 1)
                prob = prob - (row == col).astype(F32)
            coef[s, t] = prob.astype(BF)

    def text_terms(t, shards):
        total = lax.dot_general(
            coef[shards[0], t], imgs[shards[0]], TN, preferred_element_type=F32
        )
        for s in shards[1:]:
            total += lax.dot_general(
                coef[s, t], imgs[s], TN, preferred_element_type=F32
            )
        return total

    def image_terms(s, dst):
        for n in range(emb // 256):
            cols = slice(n * 256, (n + 1) * 256)
            d = jnp.dot(coef[s, 0], txts[0, :, cols], preferred_element_type=F32)
            for t in range(1, 4):
                d += jnp.dot(coef[s, t], txts[t, :, cols], preferred_element_type=F32)
            dst[:, cols] = d.astype(dst.dtype)

    quarters = [pl.ds(n * rows // 4, rows // 4) for n in range(4)]
    di_copies = [
        remote(src, dst, di_ss.at[n], di_rs.at[n], device)
        for n, (src, dst, device) in enumerate(
            (
                (di_send.at[2, half_b], di_recv.at[0, half_b], up),
                (di_send.at[1, quarters[0]], di_pass.at[quarters[0]], up),
                (di_send.at[1, quarters[1]], di_pass.at[quarters[1]], up),
                (di_send.at[2, quarters[0]], di_recv.at[0, quarters[0]], up),
                (di_send.at[2, quarters[1]], di_recv.at[0, quarters[1]], up),
                (di_send.at[0, half_a], di_recv.at[1, half_a], down),
                (di_send.at[1, quarters[2]], di_pass.at[quarters[2]], down),
                (di_send.at[1, quarters[3]], di_pass.at[quarters[3]], down),
                (di_send.at[0, quarters[2]], di_recv.at[1, quarters[2]], down),
                (di_send.at[0, quarters[3]], di_recv.at[1, quarters[3]], down),
            )
        )
    ]
    dt_copies = []
    for j in (0, 1):
        owner = y * 2 + (xh if j == 0 else jnp.where(c == 0, ox, xh))
        dt_copies.append(
            remote(
                dt_send.at[j],
                dt_recv.at[j],
                dt_ss.at[j],
                dt_rs.at[j],
                {"blk": behind, "group": owner},
            )
        )
    dt_copies.append(
        remote(dt_send.at[2], dt_recv.at[2], dt_ss.at[2], dt_rs.at[2], partner)
    )

    pairs((0, own), matching=True)
    a_copy.wait()
    for half in (0, 1):
        for n in range(width // 256):
            cols = slice(n * 256, (n + 1) * 256)
            act_t[cols, half * rows : (half + 1) * rows] = act[half, :, cols].T
    i_copies[0].wait_recv()
    i_copies[4].start()
    i_copies[2].wait_recv()
    i_copies[5].start()

    @pl.when(c == 1)
    def _():
        t_copies[1].start()

    @pl.when(c == 0)
    def _():
        landed(other_text, t_recv.at[2])
        forward_text.start()

    landed(txts.at[2], t_recv.at[0])
    pairs((0, prev))
    i_copies[1].wait_recv()
    i_copies[3].wait_recv()
    pairs((3, own), (1, own), (3, prev), (1, prev))
    d_txt[prev] = text_terms(prev, (0, 1, 3))
    landed(txts.at[3], t_recv.at[1])
    pairs((0, cross), (3, cross), (1, cross))
    d_txt[cross] = text_terms(cross, (0, 1, 3))

    @pl.when(c == 1)
    def _():
        landed(other_text, t_recv.at[2])

    pairs((3, late), (1, late))
    image_terms(3, di_send.at[2])
    di_copies[0].start()
    image_terms(1, di_send.at[0])
    di_copies[5].start()
    i_copies[4].wait_recv()
    i_copies[5].wait_recv()
    pairs((2, cross), (2, prev))
    dt_send[1] = (d_txt[cross] + text_terms(cross, (2,))).astype(BF)
    dt_copies[1].start()
    dt_send[0] = (d_txt[prev] + text_terms(prev, (2,))).astype(BF)
    dt_copies[0].start()
    pairs((2, own), (2, late), (0, late))
    image_terms(2, di_send.at[1])
    for n in (1, 6, 2, 7):
        di_copies[n].start()
    d_txt[late] = text_terms(late, (0, 1, 2, 3))

    @pl.when(c == 0)
    def _():
        landed(dt_recv.at[1], dt_rs.at[1])
        dt_send[2] = (d_txt[late] + dt_recv[1].astype(F32)).astype(BF)
        dt_copies[2].start()

    @pl.when(c == 1)
    def _():
        dt_send[2] = d_txt[late].astype(BF)
        dt_copies[2].start()

    def head_backward(t, total):
        place = jnp.where(c == t, 0, 2)

        def body(i, _):
            r = pl.ds(pl.multiple_of(i * step, step), step)
            d = sharp * total(r)
            u = unit[t, r, :]
            dot = jnp.sum(u * d, axis=-1, keepdims=True)
            at = pl.ds(pl.multiple_of(place * rows + i * step, step), step)
            dp[at, :] = ((d - u * dot) * inv_norm[t, r, :]).astype(BF)
            return 0

        lax.fori_loop(0, rows // step, body, 0, unroll=UNROLL)

    def img_total(r):
        total = d_own[r, :]
        for n in range(2):
            total += di_recv[n, r, :].astype(F32)
        return total

    d_txt[own] = text_terms(own, (0, 1, 2, 3))
    image_terms(0, d_own)
    for n, slot in ((0, 2), (2, 0), (1, 2), (3, 0)):
        arrived, onward = ((1, 3), (2, 4), (6, 8), (7, 9))[n]
        di_copies[arrived].wait_recv()
        di_send[slot, quarters[n], :] = (
            di_send[slot, quarters[n], :].astype(F32)
            + di_pass[quarters[n], :].astype(F32)
        ).astype(BF)
        di_copies[onward].start()
    for n in (0, 5, 3, 8, 4, 9):
        di_copies[n].wait_recv()
    head_backward(0, img_total)
    img_order = [lax.rem(y + d, 4) for d in (2, 1, 3, 0)]
    txt_order = (0, 2, 1, 3)

    def columns(j, core):
        n = jnp.where(core == 0, img_order[j], txt_order[j])
        return pl.ds(pl.multiple_of(n * 256, 256), 256)

    dp_copies = [
        remote(
            dp.at[pl.ds(2 * rows, rows), columns(j, oc)],
            dp.at[pl.ds(rows, rows), columns(j, oc)],
            dp_ss.at[j],
            dp_rs.at[j],
            other,
        )
        for j in range(4)
    ]

    @pl.when(c == 1)
    def _():
        for copy in dp_copies:
            copy.start()

    landed(dt_recv.at[2], dt_rs.at[2])
    landed(dt_recv.at[0], dt_rs.at[0])

    @pl.when(c == 1)
    def _():
        landed(dt_recv.at[1], dt_rs.at[1])

    both = c.astype(F32)

    def txt_total(r):
        total = d_txt[own, r, :] + dt_recv[2, r, :].astype(F32)
        total += dt_recv[0, r, :].astype(F32)
        return total + both * dt_recv[1, r, :].astype(F32)

    head_backward(1, txt_total)

    @pl.when(c == 0)
    def _():
        for copy in dp_copies:
            copy.start()


    def along_a(d):
        return device_at(
            jnp.where(c == 0, x, x + d), jnp.where(c == 0, y + d, y), z, c
        )

    pos_a = jnp.where(c == 0, y, x)
    pos_b = jnp.where(c == 0, x, y)
    fore, aft, far = (lax.rem(pos_a + d, 4) for d in (1, 3, 2))

    pieces = (
        [(wb.at[far, b], w_pass.at[b], along_a(1)) for b in (0, 1)]
        + [(wb.at[fore, b], wr1.at[0, b], along_a(1)) for b in (2, 3, 0, 1)]
        + [(wb.at[far, b], w_pass.at[b], along_a(3)) for b in (2, 3)]
        + [(wb.at[aft, b], wr1.at[1, b], along_a(3)) for b in (0, 1, 2, 3)]
    )
    w1 = [
        remote(src, dst, w1_ss.at[n], w1_rs.at[n], device)
        for n, (src, dst, device) in enumerate(pieces)
    ]

    for j in range(4):
        n = jnp.where(c == 0, img_order[j], txt_order[j])
        cols = columns(j, c)
        landed(dp.at[pl.ds(rows, rows), cols], dp_rs.at[j])
        part = jnp.dot(
            act_t[...], dp[0 : 2 * rows, cols], preferred_element_type=F32
        )
        part = part.astype(BF).reshape(8, 2, 96, 256)
        for xhi in range(2):
            for xlo in range(2):
                px = 2 * xhi + xlo
                at_a, at_b = jnp.where(c == 0, n, px), jnp.where(c == 0, px, n)
                block = part[:, xlo, :, xhi * 128 : (xhi + 1) * 128]
                wb[at_a, at_b] = block[:, 16:]
                wz[:, at_a, at_b] = block[:, :16]

        @pl.when(c == 0)
        def _():
            for n in ((0, 6, 1, 7), (2,), (8,), ())[j]:
                w1[n].start()

        @pl.when(c == 1)
        def _():
            for n in ((0, 8), (6, 2), (1,), (7,))[j]:
                w1[n].start()

    def features_backward(t, out):
        place = jnp.where(c == t, 0, 2)
        dproj = dp[pl.ds(pl.multiple_of(place * rows, rows), rows), :]
        for n in range(width // 256):
            cols = slice(n * 256, (n + 1) * 256)
            d_act[:, cols] = lax.dot_general(
                dproj, weights[t, cols, :], NT, preferred_element_type=F32
            )

        def body(i, _):
            r = pl.ds(pl.multiple_of(i * step, step), step)
            rstd = rstd_s[t, r, :]
            xhat = (feats[t, r, :].astype(F32) - mean_s[t, r, :]) * rstd
            ghat = d_act[r, :] * gains[t]
            m1 = jnp.mean(ghat, axis=-1, keepdims=True)
            m2 = jnp.mean(ghat * xhat, axis=-1, keepdims=True)
            out[r, :] = rstd * (ghat - m1 - xhat * m2)
            return 0

        lax.fori_loop(0, rows // step, body, 0, unroll=UNROLL)

    wz_copies = []
    for d in (4, 3, 5, 2, 6, 1, 7):
        wz_copies.append(
            remote(
                wz.at[lax.rem(z + d, 8)],
                rz.at[z],
                wz_ss.at[d - 1],
                wz_rs.at[z],
                device_at(x, y, z + d, c),
            )
        )
        wz_copies[-1].start()
    rz[z] = wz[z]
    features_backward(0, gi_out)
    for b, arrived, onward, chunk in (
        (0, 0, 4, fore),
        (2, 6, 10, aft),
        (1, 1, 5, fore),
        (3, 7, 11, aft),
    ):
        w1[arrived].wait_recv()
        for zz in range(8):
            wb[chunk, b, zz] = (
                wb[chunk, b, zz].astype(F32) + w_pass[b, zz].astype(F32)
            ).astype(BF)
        w1[onward].start()
        if b == 2:
            w1[3].start()
            w1[9].start()
    features_backward(1, gt_out)

    def w2_copy(b, slot, half, device):
        part = pl.ds(half * 4, 4)
        return remote(
            s1.at[b, part],
            wr2.at[slot, part],
            w2_ss.at[slot, half],
            w2_rs.at[slot, half],
            device,
        )

    def w2_start(b, half):
        device = device_at(jnp.where(c == 0, b, x), jnp.where(c == 0, y, b), z, c)
        w2_copy(b, lax.rem(b + 3 - pos_b, 4), half, device).start()

    for b, early, late_piece in ((0, 8, 4), (2, 2, 10), (1, 9, 5), (3, 3, 11)):
        w1[early].wait_recv()
        w1[late_piece].wait_recv()
        for zz in range(8):
            total = wb[pos_a, b, zz].astype(F32) + wr1[0, b, zz].astype(F32)
            s1[b, zz] = (total + wr1[1, b, zz].astype(F32)).astype(BF)

        if b == 2:
            for copy in w1:
                copy.wait_send()
            pl.semaphore_signal(
                turn, inc=1, device_id=other, device_id_type=pl.DeviceIdType.MESH
            )

    pl.semaphore_wait(turn, 1)
    for half in (0, 1):
        for b in (0, 2, 1, 3):

            @pl.when(pos_b != b)
            def _():
                w2_start(b, half)

    for d in range(1, 8):
        src = lax.rem(z + d, 8)
        landed(rz.at[src], wz_rs.at[src])
    for a in range(4):
        for b in range(4):
            total = rz[0, a, b].astype(F32)
            for zs in range(1, 8):
                total += rz[zs, a, b].astype(F32)
            sa[a, b] = total.astype(BF)
    small_copies = [
        remote(
            sa.at[lax.rem(pos_a + d, 4)],
            ra.at[d - 1],
            ra_ss.at[d - 1],
            ra_rs.at[d - 1],
            along_a(d),
        )
        for d in (2, 1, 3)
    ]
    for copy in small_copies:
        copy.start()

    def w3_copy(zd, cd):
        if cd == 0:
            src, dst = s2.at[zd, pl.ds(0, 32)], wr3.at[c, z, pl.ds(16, 32)]
        else:
            src, dst = s2.at[zd, pl.ds(32, 48)], wr3.at[c, z]
        return remote(
            src,
            dst,
            w3_ss.at[zd, cd],
            w3_rs.at[c, z],
            {"blk": zd * 4 + xl * 2 + cd, "group": g},
        )

    for half in (0, 1):
        for d in range(3):
            w2_copy(0, d, half, other).wait_recv()
        for zd in range(half * 4, half * 4 + 4):
            total = s1[pos_b, zd].astype(F32)
            for d in range(3):
                total += wr2[d, zd].astype(F32)
            s2[zd] = total.astype(BF)
            for cd in (0, 1):

                @pl.when((zd != z) | (cd != c))
                def _():
                    w3_copy(zd, cd).start()

    @pl.when(c == 0)
    def _():
        wr3[0, z, 16:48] = s2[z, 0:32]

    @pl.when(c == 1)
    def _():
        wr3[1, z] = s2[z, 32:80]

    for d in (1, 2, 3):
        landed(ra.at[d - 1], ra_rs.at[d - 1])
    for b in range(4):
        total = sa[pos_a, b].astype(F32)
        for d in range(3):
            total += ra[d, b].astype(F32)
        sb[b] = total.astype(BF)
    for d in (2, 1, 3):
        small_copies.append(
            remote(
                sb.at[lax.rem(pos_b + d, 4)],
                rb.at[d - 1],
                rb_ss.at[d - 1],
                rb_rs.at[d - 1],
                device_at(
                    jnp.where(c == 0, x + d, x), jnp.where(c == 0, y, y + d), z, c
                ),
            )
        )
        small_copies[-1].start()
    for d in (1, 2, 3):
        landed(rb.at[d - 1], rb_rs.at[d - 1])
    total = sb[pos_b].astype(F32)
    for d in range(3):
        total += rb[d].astype(F32)
    top[c] = total
    top_copy = remote(top.at[1], top.at[1], top_sem.at[0], top_sem.at[1], other)

    @pl.when(c == 1)
    def _():
        top_copy.start()
        for t, out in ((0, wi_out), (1, wt_out)):
            for zs in range(8):

                @pl.when((zs != z) | (t == 0))
                def _():
                    landed(wr3.at[t, zs], w3_rs.at[t, zs])

            total = wr3[t, 0].astype(F32)
            for zs in range(1, 8):
                total += wr3[t, zs].astype(F32)
            out[...] = total * scale
        top_copy.wait_send()

    @pl.when(c == 0)
    def _():
        top_copy.wait_recv()
        for t, out in ((0, wi_out), (1, wt_out)):
            for zs in range(8):

                @pl.when((zs != z) | (t == 1))
                def _():
                    landed(wr3.at[t, zs, pl.ds(16, 32)], w3_rs.at[t, zs])

            total = wr3[t, 0, 16:48].astype(F32)
            for zs in range(1, 8):
                total += wr3[t, zs, 16:48].astype(F32)
            out[16:48] = total * scale
            out[0:16] = top[t] * scale

    for copy in t_copies + [direct_text] + i_copies + di_copies + dt_copies:
        copy.wait_send()
    for copy in dp_copies + wz_copies + small_copies:
        copy.wait_send()
    for half in (0, 1):
        for d in range(3):
            w2_copy(0, d, half, other).wait_send()
    for zd in range(8):
        for cd in (0, 1):

            @pl.when((zd != z) | (cd != c))
            def _():
                w3_copy(zd, cd).wait_send()


def hand_out(*refs):
    copies = []
    for n in range(4):
        parts = 4 if n < 2 else 1
        size = refs[n].shape[0] // parts
        for i in range(parts):
            part = pl.ds(i * size, size)
            copies.append(
                pltpu.make_async_copy(
                    refs[n].at[part], refs[4 + n].at[part], refs[8].at[n, i]
                )
            )
    for copy in copies:
        copy.start()
    for copy in copies:
        copy.wait()


def on_device(feat_i, feat_t, gain_i, gain_t, w_i, w_t, sharp, off):
    rows, width = feat_i.shape
    emb = w_i.shape[1]
    batch = rows * lax.axis_size("group") * lax.axis_size("blk")
    scale = math.sqrt(emb / batch)
    vmem = pl.BlockSpec(memory_space=pltpu.VMEM)
    hbm = pl.BlockSpec(memory_space=pl.ANY)
    dma = pltpu.SemaphoreType.DMA
    grads = pl.pallas_call(
        functools.partial(kernel, scale),
        name="siglip_grads",
        out_shape=(
            pltpu.VMEM((rows, width), F32),
            pltpu.VMEM((rows, width), F32),
            pltpu.VMEM((48, 128), F32),
            pltpu.VMEM((48, 128), F32),
        ),
        in_specs=[hbm] * 8,
        out_specs=(vmem, vmem, vmem, vmem),
        scratch_shapes=[
            pltpu.SMEM((1,), F32),
            pltpu.SMEM((1,), F32),
            pltpu.VMEM((2, width), F32),
            dma((4,)),
            pltpu.VMEM((2, rows, width), BF),
            pltpu.VMEM((2, width, emb), BF),
            pltpu.VMEM((2, 1, width), F32),
            pltpu.VMEM((3, rows, width), BF),
            pltpu.VMEM((width, 2 * rows), BF),
            pltpu.VMEM((2, rows, emb), F32),
            pltpu.VMEM((2, rows, 1), F32),
            pltpu.VMEM((2, rows, 1), F32),
            pltpu.VMEM((2, rows, 1), F32),
            pltpu.VMEM((4, rows, emb), BF),
            pltpu.VMEM((4, rows, emb), BF),
            pltpu.VMEM((4, 4, rows, rows), BF),
            pltpu.VMEM((rows, emb), F32),
            pltpu.VMEM((4, rows, emb), F32),
            pltpu.VMEM((3, rows, emb), BF),
            pltpu.VMEM((2, rows, emb), BF),
            pltpu.VMEM((rows, emb), BF),
            pltpu.VMEM((3, rows, emb), BF),
            pltpu.VMEM((3, rows, emb), BF),
            pltpu.VMEM((3 * rows, emb), BF),
            pltpu.VMEM((rows, width), F32),
            pltpu.VMEM((4, 4, 8, 80, 128), BF),
            pltpu.VMEM((4, 8, 80, 128), BF),
            pltpu.VMEM((2, 4, 8, 80, 128), BF),
            pltpu.VMEM((4, 8, 80, 128), BF),
            pltpu.VMEM((3, 8, 80, 128), BF),
            pltpu.VMEM((8, 80, 128), BF),
            pltpu.VMEM((2, 8, 48, 128), BF),
            pltpu.VMEM((8, 4, 4, 16, 128), BF),
            pltpu.VMEM((8, 4, 4, 16, 128), BF),
            pltpu.VMEM((4, 4, 16, 128), BF),
            pltpu.VMEM((3, 4, 16, 128), BF),
            pltpu.VMEM((4, 16, 128), BF),
            pltpu.VMEM((3, 16, 128), BF),
            pltpu.VMEM((2, 16, 128), F32),
            dma((7,)),
            dma((8,)),
            dma((3,)),
            dma((3,)),
            dma((3,)),
            dma((3,)),
            dma((2,)),
            dma((4,)),
            dma((6,)),
            dma((6,)),
            dma((3,)),
            dma((3,)),
            dma((2,)),
            dma((10,)),
            dma((10,)),
            dma((3,)),
            dma((3,)),
            dma((4,)),
            dma((4,)),
            dma((12,)),
            dma((12,)),
            dma((3, 2)),
            dma((3, 2)),
            dma((8, 2)),
            dma((2, 8)),
            pltpu.SemaphoreType.REGULAR,
        ],
        compiler_params=pltpu.CompilerParams(
            collective_id=0, has_side_effects=True, vmem_limit_bytes=54 << 20
        ),
        cost_estimate=pl.CostEstimate(
            flops=11 * 10**9, bytes_accessed=11 * 10**6, transcendentals=10**6
        ),
    )(
        sharp,
        off,
        gain_i,
        gain_t,
        feat_i,
        feat_t,
        w_i,
        w_t,
    )
    return pl.pallas_call(
        hand_out,
        name="hand_out",
        out_shape=tuple(jax.ShapeDtypeStruct(a.shape, a.dtype) for a in grads),
        in_specs=[hbm] * 4,
        out_specs=(hbm,) * 4,
        scratch_shapes=[dma((4, 4))],
        compiler_params=pltpu.CompilerParams(vmem_limit_bytes=1 << 20),
    )(*grads)


def solution(mesh):
    rows = P(("blk", "group"), None)
    return jax.shard_map(
        on_device,
        mesh=mesh,
        in_specs=(rows, rows, P(), P(), P(), P(), P(), P()),
        out_specs=(rows, rows, P("blk", "group"), P("blk", "group")),
        check_vma=False,
    )
```

```python
import functools
import math

import jax
import jax.numpy as jnp
from jax import lax
from jax.experimental import pallas as pl
from jax.experimental.pallas import tpu as pltpu
from jax.sharding import PartitionSpec as P

BF = jnp.bfloat16
UNROLL = 8
F32 = jnp.float32
NT = (((1,), (1,)), ((), ()))
TN = (((0,), (0,)), ((), ()))


def device_at(x, y, z, c):
    x, y, z = lax.rem(x, 4), lax.rem(y, 4), lax.rem(z, 8)
    return {"blk": z * 4 + lax.rem(x, 2) * 2 + c, "group": y * 2 + x // 2}


def remote(src, dst, send, recv, device):
    return pltpu.make_async_remote_copy(
        src_ref=src,
        dst_ref=dst,
        send_sem=send,
        recv_sem=recv,
        device_id=device,
        device_id_type=pl.DeviceIdType.MESH,
    )


def landed(ref, sem):
    pltpu.make_async_copy(ref, ref, sem).wait()


def kernel(
    scale,
    sharp_hbm,
    off_hbm,
    gain_i,
    gain_t,
    feat_i,
    feat_t,
    w_i,
    w_t,
    gi_out,
    gt_out,
    wi_out,
    wt_out,
    sharp_ref,
    off_ref,
    gain_v,
    small_sem,
    feats,
    weights,
    gains,
    act,
    act_t,
    unit,
    inv_norm,
    mean_s,
    rstd_s,
    imgs,
    txts,
    coef,
    d_own,
    d_txt,
    di_send,
    di_recv,
    di_pass,
    dt_send,
    dt_recv,
    dp,
    d_act,
    wb,
    w_pass,
    wr1,
    s1,
    wr2,
    s2,
    wr3,
    wz,
    rz,
    sa,
    ra,
    sb,
    rb,
    top,
    wz_ss,
    wz_rs,
    ra_ss,
    ra_rs,
    rb_ss,
    rb_rs,
    top_sem,
    load_sem,
    i_send,
    i_recv,
    t_send,
    t_recv,
    a_sem,
    di_ss,
    di_rs,
    dt_ss,
    dt_rs,
    dp_ss,
    dp_rs,
    w1_ss,
    w1_rs,
    w2_ss,
    w2_rs,
    w3_ss,
    w3_rs,
    turn,
):
    k = lax.axis_index("blk")
    g = lax.axis_index("group")
    c = lax.rem(k, 2)
    z = k // 4
    xl = lax.rem(k // 2, 2)
    y = g // 2
    xh = lax.rem(g, 2)
    x = 2 * xh + xl
    oc = 1 - c
    ox = 1 - xh
    other = {"blk": k + 1 - 2 * c, "group": g}
    partner = {"blk": k, "group": y * 2 + ox}
    behind = lax.rem(k + 31, 32)
    ahead = lax.rem(k + 1, 32)
    linked = lax.rem(k + 31 + 2 * c, 32)
    rows, width = feats.shape[1], feats.shape[2]
    emb = imgs.shape[2]

    small = [
        pltpu.make_async_copy(src, dst, small_sem.at[n])
        for n, (src, dst) in enumerate(
            (
                (gain_t, gain_v.at[1]),
                (gain_i, gain_v.at[0]),
                (sharp_hbm, sharp_ref),
                (off_hbm, off_ref),
            )
        )
    ]
    for load in small:
        load.start()
    loads = [
        pltpu.make_async_copy(feat_t, feats.at[1], load_sem.at[0]),
        pltpu.make_async_copy(w_t, weights.at[1], load_sem.at[1]),
        pltpu.make_async_copy(feat_i, feats.at[0], load_sem.at[2]),
        pltpu.make_async_copy(w_i, weights.at[0], load_sem.at[3]),
    ]
    for n in (0, 2, 1):
        loads[n].start()

    barrier = pltpu.get_barrier_semaphore()
    partners = [device_at(x, y + d, z, c) for d in (1, 2, 3)]
    partners += [device_at(x + d, y, z, c) for d in (1, 2, 3)]
    partners += [device_at(x, y, z + d, c) for d in range(1, 8)]
    partners += [device_at(x, y, z + d, oc) for d in range(8)]
    partners += [{"blk": linked, "group": y * 2 + j} for j in (0, 1)]
    for device in partners:
        pl.semaphore_signal(
            barrier, inc=1, device_id=device, device_id_type=pl.DeviceIdType.MESH
        )
    for load in small:
        load.wait()
    gains[0] = gain_v[0].reshape(1, width)
    gains[1] = gain_v[1].reshape(1, width)

    step = 32

    def normalize(t, wait_features):
        wait_features.wait()
        place = jnp.where(c == t, 0, 2)

        def body(i, _):
            r = pl.ds(pl.multiple_of(i * step, step), step)
            v = feats[t, r, :].astype(F32)
            mu = jnp.mean(v, axis=-1, keepdims=True)
            cen = v - mu
            rstd = lax.rsqrt(jnp.mean(cen * cen, axis=-1, keepdims=True) + 1e-06)
            mean_s[t, r, :] = mu
            rstd_s[t, r, :] = rstd
            act[place, r, :] = (cen * rstd * gains[t]).astype(BF)
            return 0

        lax.fori_loop(0, rows // step, body, 0, unroll=UNROLL)

    def project(t, wait_weights, dst):
        wait_weights.wait()
        if t == 1:
            loads[3].start()
        place = jnp.where(c == t, 0, 2)
        for n in range(emb // 256):
            cols = slice(n * 256, (n + 1) * 256)
            unit[t, :, cols] = jnp.dot(
                act[place], weights[t, :, cols], preferred_element_type=F32
            )

        def body(i, _):
            r = pl.ds(pl.multiple_of(i * step, step), step)
            p = unit[t, r, :]
            inv = lax.rsqrt(jnp.sum(p * p, axis=-1, keepdims=True) + 1e-06)
            u = p * inv
            unit[t, r, :] = u
            inv_norm[t, r, :] = inv
            dst[r, :] = u.astype(BF)
            return 0

        lax.fori_loop(0, rows // step, body, 0, unroll=UNROLL)

    normalize(1, loads[0])
    normalize(0, loads[2])
    project(1, loads[1], txts.at[0])
    pl.semaphore_wait(barrier, 23)

    own_text = txts.at[0]
    other_text = txts.at[1]
    t_copies = [
        remote(
            own_text,
            txts.at[2],
            t_send.at[0],
            t_recv.at[0],
            {"blk": ahead, "group": g},
        ),
        remote(own_text, other_text, t_send.at[1], t_recv.at[2], partner),
    ]
    direct_text = remote(
        own_text,
        txts.at[3],
        t_send.at[2],
        t_recv.at[1],
        {"blk": ahead, "group": y * 2 + ox},
    )
    forward_text = remote(
        other_text,
        txts.at[3],
        t_send.at[2],
        t_recv.at[1],
        {"blk": ahead, "group": g},
    )

    @pl.when(c == 1)
    def _():
        direct_text.start()

    t_copies[0].start()

    @pl.when(c == 0)
    def _():
        t_copies[1].start()

    project(0, loads[3], imgs.at[0])
    half_a, half_b = pl.ds(0, rows // 2), pl.ds(rows // 2, rows // 2)
    up, down = device_at(x, y + 1, z, c), device_at(x, y + 3, z, c)
    i_copies = [
        remote(
            imgs.at[src, part], imgs.at[dst, part], i_send.at[n], i_recv.at[n], device
        )
        for n, (src, dst, part, device) in enumerate(
            (
                (0, 1, half_a, up),
                (0, 1, half_b, up),
                (0, 3, half_b, down),
                (0, 3, half_a, down),
                (1, 2, half_a, up),
                (3, 2, half_b, down),
            )
        )
    ]
    for n in (0, 2, 1, 3):
        i_copies[n].start()
    a_copy = remote(act.at[2], act.at[1], a_sem.at[0], a_sem.at[1], other)
    a_copy.start()

    sharp = sharp_ref[0]
    off = off_ref[0]
    own, late, prev, cross = 0, 1, 2, 3

    def pairs(*todo, matching=False):
        for s, t in todo:
            sim = lax.dot_general(imgs[s], txts[t], NT, preferred_element_type=F32)
            prob = jax.nn.sigmoid(sharp * sim + off)
            if matching:
                row = lax.broadcasted_iota(jnp.int32, (rows, rows), 0)
                col = lax.broadcasted_iota(jnp.int32, (rows, rows), 1)
                prob = prob - (row == col).astype(F32)
            coef[s, t] = prob.astype(BF)

    def text_terms(t, shards):
        total = lax.dot_general(
            coef[shards[0], t], imgs[shards[0]], TN, preferred_element_type=F32
        )
        for s in shards[1:]:
            total += lax.dot_general(
                coef[s, t], imgs[s], TN, preferred_element_type=F32
            )
        return total

    def image_terms(s, dst):
        for n in range(emb // 256):
            cols = slice(n * 256, (n + 1) * 256)
            d = jnp.dot(coef[s, 0], txts[0, :, cols], preferred_element_type=F32)
            for t in range(1, 4):
                d += jnp.dot(coef[s, t], txts[t, :, cols], preferred_element_type=F32)
            dst[:, cols] = d.astype(dst.dtype)

    quarters = [pl.ds(n * rows // 4, rows // 4) for n in range(4)]
    di_copies = [
        remote(src, dst, di_ss.at[n], di_rs.at[n], device)
        for n, (src, dst, device) in enumerate(
            (
                (di_send.at[2, half_b], di_recv.at[0, half_b], up),
                (di_send.at[1, quarters[0]], di_pass.at[quarters[0]], up),
                (di_send.at[1, quarters[1]], di_pass.at[quarters[1]], up),
                (di_send.at[2, quarters[0]], di_recv.at[0, quarters[0]], up),
                (di_send.at[2, quarters[1]], di_recv.at[0, quarters[1]], up),
                (di_send.at[0, half_a], di_recv.at[1, half_a], down),
                (di_send.at[1, quarters[2]], di_pass.at[quarters[2]], down),
                (di_send.at[1, quarters[3]], di_pass.at[quarters[3]], down),
                (di_send.at[0, quarters[2]], di_recv.at[1, quarters[2]], down),
                (di_send.at[0, quarters[3]], di_recv.at[1, quarters[3]], down),
            )
        )
    ]
    dt_copies = []
    for j in (0, 1):
        owner = y * 2 + (xh if j == 0 else jnp.where(c == 0, ox, xh))
        dt_copies.append(
            remote(
                dt_send.at[j],
                dt_recv.at[j],
                dt_ss.at[j],
                dt_rs.at[j],
                {"blk": behind, "group": owner},
            )
        )
    dt_copies.append(
        remote(dt_send.at[2], dt_recv.at[2], dt_ss.at[2], dt_rs.at[2], partner)
    )

    pairs((0, own), matching=True)
    a_copy.wait()
    for half in (0, 1):
        for n in range(width // 256):
            cols = slice(n * 256, (n + 1) * 256)
            act_t[cols, half * rows : (half + 1) * rows] = act[half, :, cols].T
    i_copies[0].wait_recv()
    i_copies[4].start()
    i_copies[2].wait_recv()
    i_copies[5].start()

    @pl.when(c == 1)
    def _():
        t_copies[1].start()

    @pl.when(c == 0)
    def _():
        landed(other_text, t_recv.at[2])
        forward_text.start()

    landed(txts.at[2], t_recv.at[0])
    pairs((0, prev))
    i_copies[1].wait_recv()
    i_copies[3].wait_recv()
    pairs((3, own), (1, own), (3, prev), (1, prev))
    d_txt[prev] = text_terms(prev, (0, 1, 3))
    landed(txts.at[3], t_recv.at[1])
    pairs((0, cross), (3, cross), (1, cross))
    d_txt[cross] = text_terms(cross, (0, 1, 3))

    @pl.when(c == 1)
    def _():
        landed(other_text, t_recv.at[2])

    pairs((3, late), (1, late))
    image_terms(3, di_send.at[2])
    di_copies[0].start()
    image_terms(1, di_send.at[0])
    di_copies[5].start()
    i_copies[4].wait_recv()
    i_copies[5].wait_recv()
    pairs((2, cross), (2, prev))
    dt_send[1] = (d_txt[cross] + text_terms(cross, (2,))).astype(BF)
    dt_copies[1].start()
    dt_send[0] = (d_txt[prev] + text_terms(prev, (2,))).astype(BF)
    dt_copies[0].start()
    pairs((2, own), (2, late), (0, late))
    image_terms(2, di_send.at[1])
    for n in (1, 6, 2, 7):
        di_copies[n].start()
    d_txt[late] = text_terms(late, (0, 1, 2, 3))

    @pl.when(c == 0)
    def _():
        landed(dt_recv.at[1], dt_rs.at[1])
        dt_send[2] = (d_txt[late] + dt_recv[1].astype(F32)).astype(BF)
        dt_copies[2].start()

    @pl.when(c == 1)
    def _():
        dt_send[2] = d_txt[late].astype(BF)
        dt_copies[2].start()

    def head_backward(t, total):
        place = jnp.where(c == t, 0, 2)

        def body(i, _):
            r = pl.ds(pl.multiple_of(i * step, step), step)
            d = sharp * total(r)
            u = unit[t, r, :]
            dot = jnp.sum(u * d, axis=-1, keepdims=True)
            at = pl.ds(pl.multiple_of(place * rows + i * step, step), step)
            dp[at, :] = ((d - u * dot) * inv_norm[t, r, :]).astype(BF)
            return 0

        lax.fori_loop(0, rows // step, body, 0, unroll=UNROLL)

    def img_total(r):
        total = d_own[r, :]
        for n in range(2):
            total += di_recv[n, r, :].astype(F32)
        return total

    d_txt[own] = text_terms(own, (0, 1, 2, 3))
    image_terms(0, d_own)
    for n, slot in ((0, 2), (2, 0), (1, 2), (3, 0)):
        arrived, onward = ((1, 3), (2, 4), (6, 8), (7, 9))[n]
        di_copies[arrived].wait_recv()
        di_send[slot, quarters[n], :] = (
            di_send[slot, quarters[n], :].astype(F32)
            + di_pass[quarters[n], :].astype(F32)
        ).astype(BF)
        di_copies[onward].start()
    for n in (0, 5, 3, 8, 4, 9):
        di_copies[n].wait_recv()
    head_backward(0, img_total)
    img_order = [lax.rem(y + d, 4) for d in (2, 1, 3, 0)]
    txt_order = (0, 2, 1, 3)

    def columns(j, core):
        n = jnp.where(core == 0, img_order[j], txt_order[j])
        return pl.ds(pl.multiple_of(n * 256, 256), 256)

    dp_copies = [
        remote(
            dp.at[pl.ds(2 * rows, rows), columns(j, oc)],
            dp.at[pl.ds(rows, rows), columns(j, oc)],
            dp_ss.at[j],
            dp_rs.at[j],
            other,
        )
        for j in range(4)
    ]

    @pl.when(c == 1)
    def _():
        for copy in dp_copies:
            copy.start()

    def along_a(d):
        return device_at(
            jnp.where(c == 0, x, x + d), jnp.where(c == 0, y + d, y), z, c
        )

    pos_a = jnp.where(c == 0, y, x)
    pos_b = jnp.where(c == 0, x, y)
    fore, aft, far = (lax.rem(pos_a + d, 4) for d in (1, 3, 2))

    pieces = (
        [(wb.at[far, b], w_pass.at[b], along_a(1)) for b in (0, 1)]
        + [(wb.at[fore, b], wr1.at[0, b], along_a(1)) for b in (2, 3, 0, 1)]
        + [(wb.at[far, b], w_pass.at[b], along_a(3)) for b in (2, 3)]
        + [(wb.at[aft, b], wr1.at[1, b], along_a(3)) for b in (0, 1, 2, 3)]
    )
    w1 = [
        remote(src, dst, w1_ss.at[n], w1_rs.at[n], device)
        for n, (src, dst, device) in enumerate(pieces)
    ]

    def weight_terms(j):
        n = jnp.where(c == 0, img_order[j], txt_order[j])
        cols = columns(j, c)
        landed(dp.at[pl.ds(rows, rows), cols], dp_rs.at[j])
        part = jnp.dot(
            act_t[...], dp[0 : 2 * rows, cols], preferred_element_type=F32
        )
        part = part.astype(BF).reshape(8, 2, 96, 256)
        for xhi in range(2):
            for xlo in range(2):
                px = 2 * xhi + xlo
                at_a, at_b = jnp.where(c == 0, n, px), jnp.where(c == 0, px, n)
                block = part[:, xlo, :, xhi * 128 : (xhi + 1) * 128]
                wb[at_a, at_b] = block[:, 16:]
                wz[:, at_a, at_b] = block[:, :16]

        @pl.when(c == 0)
        def _():
            for n in ((0, 6, 1, 7), (2,), (8,), ())[j]:
                w1[n].start()

        @pl.when(c == 1)
        def _():
            for n in ((0, 8), (6, 2), (1,), (7,))[j]:
                w1[n].start()

    def features_backward(t, out):
        place = jnp.where(c == t, 0, 2)
        dproj = dp[pl.ds(pl.multiple_of(place * rows, rows), rows), :]
        for n in range(width // 256):
            cols = slice(n * 256, (n + 1) * 256)
            d_act[:, cols] = lax.dot_general(
                dproj, weights[t, cols, :], NT, preferred_element_type=F32
            )

        def body(i, _):
            r = pl.ds(pl.multiple_of(i * step, step), step)
            rstd = rstd_s[t, r, :]
            xhat = (feats[t, r, :].astype(F32) - mean_s[t, r, :]) * rstd
            ghat = d_act[r, :] * gains[t]
            m1 = jnp.mean(ghat, axis=-1, keepdims=True)
            m2 = jnp.mean(ghat * xhat, axis=-1, keepdims=True)
            out[r, :] = rstd * (ghat - m1 - xhat * m2)
            return 0

        lax.fori_loop(0, rows // step, body, 0, unroll=UNROLL)

    @pl.when(c == 0)
    def _():
        weight_terms(0)

    landed(dt_recv.at[2], dt_rs.at[2])
    landed(dt_recv.at[0], dt_rs.at[0])

    @pl.when(c == 1)
    def _():
        landed(dt_recv.at[1], dt_rs.at[1])

    both = c.astype(F32)

    def txt_total(r):
        total = d_txt[own, r, :] + dt_recv[2, r, :].astype(F32)
        total += dt_recv[0, r, :].astype(F32)
        return total + both * dt_recv[1, r, :].astype(F32)

    head_backward(1, txt_total)

    @pl.when(c == 0)
    def _():
        for copy in dp_copies:
            copy.start()


    @pl.when(c == 1)
    def _():
        weight_terms(0)

    for j in (1, 2, 3):
        weight_terms(j)

    wz_copies = []
    for d in (4, 3, 5, 2, 6, 1, 7):
        wz_copies.append(
            remote(
                wz.at[lax.rem(z + d, 8)],
                rz.at[z],
                wz_ss.at[d - 1],
                wz_rs.at[z],
                device_at(x, y, z + d, c),
            )
        )
        wz_copies[-1].start()
    rz[z] = wz[z]
    features_backward(0, gi_out)
    for b, arrived, onward, chunk in (
        (0, 0, 4, fore),
        (2, 6, 10, aft),
        (1, 1, 5, fore),
        (3, 7, 11, aft),
    ):
        w1[arrived].wait_recv()
        for zz in range(8):
            wb[chunk, b, zz] = (
                wb[chunk, b, zz].astype(F32) + w_pass[b, zz].astype(F32)
            ).astype(BF)
        w1[onward].start()
        if b == 2:
            w1[3].start()
            w1[9].start()
    features_backward(1, gt_out)

    def w2_copy(b, slot, half, device):
        part = pl.ds(half * 4, 4)
        return remote(
            s1.at[b, part],
            wr2.at[slot, part],
            w2_ss.at[slot, half],
            w2_rs.at[slot, half],
            device,
        )

    def w2_start(b, half):
        device = device_at(jnp.where(c == 0, b, x), jnp.where(c == 0, y, b), z, c)
        w2_copy(b, lax.rem(b + 3 - pos_b, 4), half, device).start()

    for b, early, late_piece in ((0, 8, 4), (2, 2, 10), (1, 9, 5), (3, 3, 11)):
        w1[early].wait_recv()
        w1[late_piece].wait_recv()
        for zz in range(8):
            total = wb[pos_a, b, zz].astype(F32) + wr1[0, b, zz].astype(F32)
            s1[b, zz] = (total + wr1[1, b, zz].astype(F32)).astype(BF)

        if b == 2:
            for copy in w1:
                copy.wait_send()
            pl.semaphore_signal(
                turn, inc=1, device_id=other, device_id_type=pl.DeviceIdType.MESH
            )

    pl.semaphore_wait(turn, 1)
    for half in (0, 1):
        for b in (0, 2, 1, 3):

            @pl.when(pos_b != b)
            def _():
                w2_start(b, half)

    for d in range(1, 8):
        src = lax.rem(z + d, 8)
        landed(rz.at[src], wz_rs.at[src])
    for a in range(4):
        for b in range(4):
            total = rz[0, a, b].astype(F32)
            for zs in range(1, 8):
                total += rz[zs, a, b].astype(F32)
            sa[a, b] = total.astype(BF)
    small_copies = [
        remote(
            sa.at[lax.rem(pos_a + d, 4)],
            ra.at[d - 1],
            ra_ss.at[d - 1],
            ra_rs.at[d - 1],
            along_a(d),
        )
        for d in (2, 1, 3)
    ]
    for copy in small_copies:
        copy.start()

    def w3_copy(zd, cd):
        if cd == 0:
            src, dst = s2.at[zd, pl.ds(0, 32)], wr3.at[c, z, pl.ds(16, 32)]
        else:
            src, dst = s2.at[zd, pl.ds(32, 48)], wr3.at[c, z]
        return remote(
            src,
            dst,
            w3_ss.at[zd, cd],
            w3_rs.at[c, z],
            {"blk": zd * 4 + xl * 2 + cd, "group": g},
        )

    for half in (0, 1):
        for d in range(3):
            w2_copy(0, d, half, other).wait_recv()
        for zd in range(half * 4, half * 4 + 4):
            total = s1[pos_b, zd].astype(F32)
            for d in range(3):
                total += wr2[d, zd].astype(F32)
            s2[zd] = total.astype(BF)
            for cd in (0, 1):

                @pl.when((zd != z) | (cd != c))
                def _():
                    w3_copy(zd, cd).start()

    @pl.when(c == 0)
    def _():
        wr3[0, z, 16:48] = s2[z, 0:32]

    @pl.when(c == 1)
    def _():
        wr3[1, z] = s2[z, 32:80]

    for d in (1, 2, 3):
        landed(ra.at[d - 1], ra_rs.at[d - 1])
    for b in range(4):
        total = sa[pos_a, b].astype(F32)
        for d in range(3):
            total += ra[d, b].astype(F32)
        sb[b] = total.astype(BF)
    for d in (2, 1, 3):
        small_copies.append(
            remote(
                sb.at[lax.rem(pos_b + d, 4)],
                rb.at[d - 1],
                rb_ss.at[d - 1],
                rb_rs.at[d - 1],
                device_at(
                    jnp.where(c == 0, x + d, x), jnp.where(c == 0, y, y + d), z, c
                ),
            )
        )
        small_copies[-1].start()
    for d in (1, 2, 3):
        landed(rb.at[d - 1], rb_rs.at[d - 1])
    total = sb[pos_b].astype(F32)
    for d in range(3):
        total += rb[d].astype(F32)
    top[c] = total
    top_copy = remote(top.at[1], top.at[1], top_sem.at[0], top_sem.at[1], other)

    @pl.when(c == 1)
    def _():
        top_copy.start()
        for t, out in ((0, wi_out), (1, wt_out)):
            for zs in range(8):

                @pl.when((zs != z) | (t == 0))
                def _():
                    landed(wr3.at[t, zs], w3_rs.at[t, zs])

            total = wr3[t, 0].astype(F32)
            for zs in range(1, 8):
                total += wr3[t, zs].astype(F32)
            out[...] = total * scale
        top_copy.wait_send()

    @pl.when(c == 0)
    def _():
        top_copy.wait_recv()
        for t, out in ((0, wi_out), (1, wt_out)):
            for zs in range(8):

                @pl.when((zs != z) | (t == 1))
                def _():
                    landed(wr3.at[t, zs, pl.ds(16, 32)], w3_rs.at[t, zs])

            total = wr3[t, 0, 16:48].astype(F32)
            for zs in range(1, 8):
                total += wr3[t, zs, 16:48].astype(F32)
            out[16:48] = total * scale
            out[0:16] = top[t] * scale

    for copy in t_copies + [direct_text] + i_copies + di_copies + dt_copies:
        copy.wait_send()
    for copy in dp_copies + wz_copies + small_copies:
        copy.wait_send()
    for half in (0, 1):
        for d in range(3):
            w2_copy(0, d, half, other).wait_send()
    for zd in range(8):
        for cd in (0, 1):

            @pl.when((zd != z) | (cd != c))
            def _():
                w3_copy(zd, cd).wait_send()


def hand_out(*refs):
    copies = []
    for n in range(4):
        parts = 4 if n < 2 else 1
        size = refs[n].shape[0] // parts
        for i in range(parts):
            part = pl.ds(i * size, size)
            copies.append(
                pltpu.make_async_copy(
                    refs[n].at[part], refs[4 + n].at[part], refs[8].at[n, i]
                )
            )
    for copy in copies:
        copy.start()
    for copy in copies:
        copy.wait()


def on_device(feat_i, feat_t, gain_i, gain_t, w_i, w_t, sharp, off):
    rows, width = feat_i.shape
    emb = w_i.shape[1]
    batch = rows * lax.axis_size("group") * lax.axis_size("blk")
    scale = math.sqrt(emb / batch)
    vmem = pl.BlockSpec(memory_space=pltpu.VMEM)
    hbm = pl.BlockSpec(memory_space=pl.ANY)
    dma = pltpu.SemaphoreType.DMA
    grads = pl.pallas_call(
        functools.partial(kernel, scale),
        name="siglip_grads",
        out_shape=(
            pltpu.VMEM((rows, width), F32),
            pltpu.VMEM((rows, width), F32),
            pltpu.VMEM((48, 128), F32),
            pltpu.VMEM((48, 128), F32),
        ),
        in_specs=[hbm] * 8,
        out_specs=(vmem, vmem, vmem, vmem),
        scratch_shapes=[
            pltpu.SMEM((1,), F32),
            pltpu.SMEM((1,), F32),
            pltpu.VMEM((2, width), F32),
            dma((4,)),
            pltpu.VMEM((2, rows, width), BF),
            pltpu.VMEM((2, width, emb), BF),
            pltpu.VMEM((2, 1, width), F32),
            pltpu.VMEM((3, rows, width), BF),
            pltpu.VMEM((width, 2 * rows), BF),
            pltpu.VMEM((2, rows, emb), F32),
            pltpu.VMEM((2, rows, 1), F32),
            pltpu.VMEM((2, rows, 1), F32),
            pltpu.VMEM((2, rows, 1), F32),
            pltpu.VMEM((4, rows, emb), BF),
            pltpu.VMEM((4, rows, emb), BF),
            pltpu.VMEM((4, 4, rows, rows), BF),
            pltpu.VMEM((rows, emb), F32),
            pltpu.VMEM((4, rows, emb), F32),
            pltpu.VMEM((3, rows, emb), BF),
            pltpu.VMEM((2, rows, emb), BF),
            pltpu.VMEM((rows, emb), BF),
            pltpu.VMEM((3, rows, emb), BF),
            pltpu.VMEM((3, rows, emb), BF),
            pltpu.VMEM((3 * rows, emb), BF),
            pltpu.VMEM((rows, width), F32),
            pltpu.VMEM((4, 4, 8, 80, 128), BF),
            pltpu.VMEM((4, 8, 80, 128), BF),
            pltpu.VMEM((2, 4, 8, 80, 128), BF),
            pltpu.VMEM((4, 8, 80, 128), BF),
            pltpu.VMEM((3, 8, 80, 128), BF),
            pltpu.VMEM((8, 80, 128), BF),
            pltpu.VMEM((2, 8, 48, 128), BF),
            pltpu.VMEM((8, 4, 4, 16, 128), BF),
            pltpu.VMEM((8, 4, 4, 16, 128), BF),
            pltpu.VMEM((4, 4, 16, 128), BF),
            pltpu.VMEM((3, 4, 16, 128), BF),
            pltpu.VMEM((4, 16, 128), BF),
            pltpu.VMEM((3, 16, 128), BF),
            pltpu.VMEM((2, 16, 128), F32),
            dma((7,)),
            dma((8,)),
            dma((3,)),
            dma((3,)),
            dma((3,)),
            dma((3,)),
            dma((2,)),
            dma((4,)),
            dma((6,)),
            dma((6,)),
            dma((3,)),
            dma((3,)),
            dma((2,)),
            dma((10,)),
            dma((10,)),
            dma((3,)),
            dma((3,)),
            dma((4,)),
            dma((4,)),
            dma((12,)),
            dma((12,)),
            dma((3, 2)),
            dma((3, 2)),
            dma((8, 2)),
            dma((2, 8)),
            pltpu.SemaphoreType.REGULAR,
        ],
        compiler_params=pltpu.CompilerParams(
            collective_id=0, has_side_effects=True, vmem_limit_bytes=54 << 20
        ),
        cost_estimate=pl.CostEstimate(
            flops=11 * 10**9, bytes_accessed=11 * 10**6, transcendentals=10**6
        ),
    )(
        sharp,
        off,
        gain_i,
        gain_t,
        feat_i,
        feat_t,
        w_i,
        w_t,
    )
    return pl.pallas_call(
        hand_out,
        name="hand_out",
        out_shape=tuple(jax.ShapeDtypeStruct(a.shape, a.dtype) for a in grads),
        in_specs=[hbm] * 4,
        out_specs=(hbm,) * 4,
        scratch_shapes=[dma((4, 4))],
        compiler_params=pltpu.CompilerParams(vmem_limit_bytes=1 << 20),
    )(*grads)


def solution(mesh):
    rows = P(("blk", "group"), None)
    return jax.shard_map(
        on_device,
        mesh=mesh,
        in_specs=(rows, rows, P(), P(), P(), P(), P(), P()),
        out_specs=(rows, rows, P("blk", "group"), P("blk", "group")),
        check_vma=False,
    )
```
